512 devices in a mesh: cuts: 64 (over z, x_lo, core), event: 8 (over y, x_hi).
Axes of the slice: x: 4 (x_hi: 2, x_lo: 2; x = x_hi * 2 + x_lo), y: 4, z: 16, core: 2. Of those that a mesh axis runs over, the one named last changes fastest.
Arguments:
- adjoint_now: float32 [8, 17, 33, 8192], P('event', None, None, 'cuts'), may hold values from -6 to 6
- adjoint_prev: float32 [8, 17, 33, 8192], P('event', None, None, 'cuts'), may hold values from -6 to 6
- backward_now: float32 [8, 17, 33, 8192], P('event', None, None, 'cuts'), may hold values from -6 to 6
- backward_prev: float32 [8, 17, 33, 8192], P('event', None, None, 'cuts'), may hold values from -6 to 6
- kappa: float32 [17, 33, 8192], P(None, None, 'cuts'), may hold values from 1 to 4
- density: float32 [17, 33, 8192], P(None, None, 'cuts'), may hold values from 1 to 2
- edge_flip: int32 [64], P('cuts'), may hold values 0 or 1
- receiver_index: int32 [1024], P('cuts'), may hold values from 0 to 71807
- adjoint_source: float32 [8, 2, 1024], P('event', None, 'cuts'), may hold values from -150 to 150
Outputs:
- adjoint_final: float32 [8, 17, 33, 8192], P('event', None, None, 'cuts')
- adjoint_last: float32 [8, 17, 33, 8192], P('event', None, None, 'cuts')
- backward_final: float32 [8, 17, 33, 8192], P('event', None, None, 'cuts')
- backward_last: float32 [8, 17, 33, 8192], P('event', None, None, 'cuts')
- smoothed_kernel: float32 [17, 33, 8192], P(None, None, 'cuts')
The draws below stay inside these ranges and needn't reach their ends.
Inputs may be any that keep to these rules, and one draw needn't show every extreme that they name: receiver_index[r] names a point of slice r // 16; several receivers may share a point. `edge_flip`: 1 where the interface after a slice reverses the second dimension.
All inputs are finite; a program needn't handle non-finite values. No bound on the sum of `edge_flip` on one device may be relied on, other than what follows from the above.
Results may differ from the reference program's by a relative error of at most 0.00012.
Values sent between devices are 32-bit elements; how exact they have to be, the bound alone decides.
No kernel may reach another device: no remote copies, remote signals or barrier semaphores. Data moves between devices by JAX's collectives and lax.ppermute only.
A program may use at most 64 MiB of HBM per device.

```python
import math
import jax
import jax.numpy as jnp
import numpy as np
from jax import lax

EX = 32
EY = 8
EZ = 4
RECV = 16
STEPS = 2
ZP = 17
YP = 33
XL = 128
NX = 8192
EVENTS = 8
RECVS = 1024
N_CUTS = 64


def with_ends(entries, rng, least, high):
    place = [jax.random.randint(jax.random.fold_in(rng, axis), (), 0, length) for axis, length in enumerate(entries.shape)]
    main_axis = entries.shape.index(max(entries.shape))
    beside = place[:main_axis] + [(place[main_axis] + 1) % entries.shape[main_axis]] + place[main_axis + 1:]
    return entries.at[tuple(place)].set(least).at[tuple(beside)].set(high)


def shard_levels(rng, shape, split, least, top_value):
    def one(dim, blocks):
        steps = jax.random.uniform(jax.random.fold_in(jax.random.fold_in(rng, 6), dim), (blocks,), jnp.float32, least / len(split), top_value / len(split))
        return jnp.repeat(jnp.exp(steps), shape[dim] // blocks).reshape((-1,) + (1,) * (len(shape) - dim - 1))

    level = one(*split[0])
    for cut in split[1:]:
        level = level * one(*cut)
    return level


def noise(rng, extent, spread, most, split=(), held_as=jnp.bfloat16):
    level = shard_levels(rng, extent, split, -0.22, 0.18) if split else 1.0
    entries = jax.random.normal(rng, extent, jnp.float32) * spread * level
    return jnp.minimum(jnp.maximum(entries, -most), most).astype(held_as)


def setup_inputs(seed: int = 0) -> dict:
    seeds = jax.random.split(jax.random.key(seed), 10)
    return {
        "adjoint_now": noise(seeds[0], (EVENTS, ZP, YP, NX), 1.0, 6.0, ((0, 8), (3, 64)), jnp.float32),
        "adjoint_prev": noise(seeds[1], (EVENTS, ZP, YP, NX), 1.0, 6.0, ((0, 8), (3, 64)), jnp.float32),
        "backward_now": noise(seeds[2], (EVENTS, ZP, YP, NX), 1.0, 6.0, ((0, 8), (3, 64)), jnp.float32),
        "backward_prev": noise(seeds[3], (EVENTS, ZP, YP, NX), 1.0, 6.0, ((0, 8), (3, 64)), jnp.float32),
        "kappa": jnp.clip(jnp.exp(math.log(4.0) - 1.3862944 * jax.random.uniform(seeds[4], (ZP, YP, NX), jnp.float32) ** shard_levels(seeds[4], (ZP, YP, NX), ((2, 64),), -0.2, 0.2)), 1.0, 4.0),
        "density": jnp.clip(jnp.exp(math.log(2.0) - 0.6931472 * jax.random.uniform(seeds[5], (ZP, YP, NX), jnp.float32) ** shard_levels(seeds[5], (ZP, YP, NX), ((2, 64),), -0.2, 0.2)), 1.0, 2.0),
        "edge_flip": with_ends((jax.random.randint(seeds[6], (N_CUTS,), 0, 2) < 1).astype(jnp.int32), jax.random.fold_in(seeds[6], 1), 0, 1),
        "receiver_index": with_ends(jax.random.randint(seeds[7], (RECVS,), 0, ZP * YP * XL), jax.random.fold_in(seeds[7], 1), 0, (ZP * YP * XL) - 1).astype(jnp.int32),
        "adjoint_source": noise(seeds[8], (EVENTS, STEPS, RECVS), 30.0, 150.0, ((0, 8), (2, 64)), jnp.float32),
    }


DT2 = 0.003
SIGMA_Y = 1.0
HIGHEST = lax.Precision.HIGHEST

def gll_tables():
    gll_nodes = np.array([-1.0, -np.sqrt(3.0 / 7.0), 0.0, np.sqrt(3.0 / 7.0), 1.0])
    weights = np.array([0.1, 49.0 / 90.0, 32.0 / 45.0, 49.0 / 90.0, 0.1])
    derivative = np.zeros((5, 5))
    for a in range(5):
        for b in range(5):
            summed = 0.0
            for m in range(5):
                if m == b:
                    continue
                factor = 1.0 / (gll_nodes[b] - gll_nodes[m])
                for k in range(5):
                    if k == b or k == m:
                        continue
                    factor = factor * (gll_nodes[a] - gll_nodes[k]) / (gll_nodes[b] - gll_nodes[k])
                summed = summed + factor
            derivative[a, b] = summed
    return (weights, derivative)

def line_weights(element_count):
    weights, derivative = gll_tables()
    summed = np.zeros(4 * element_count + 1)
    for element in range(element_count):
        summed[4 * element:4 * element + 5] += weights
    return summed

def loop_weights(element_count):
    summed = line_weights(element_count)
    summed[0] += summed[-1]
    return summed[:-1]

def element_tables(element_count):
    weights, derivative = gll_tables()
    applied = np.zeros((5 * element_count, 4 * element_count + 1))
    picked = np.zeros((5 * element_count, 4 * element_count + 1))
    for element in range(element_count):
        applied[5 * element:5 * element + 5, 4 * element:4 * element + 5] = derivative
        picked[5 * element:5 * element + 5, 4 * element:4 * element + 5] = np.eye(5)
    node_weights = np.tile(weights, element_count)
    return (jnp.asarray(applied, jnp.float32), jnp.asarray(picked, jnp.float32), jnp.asarray(node_weights, jnp.float32))

def build_tables(count_ext, count_x, count_y, count_z):
    return (element_tables(count_ext), element_tables(count_y), element_tables(count_z), jnp.asarray(loop_weights(count_x), jnp.float32), jnp.asarray(line_weights(count_y), jnp.float32), jnp.asarray(line_weights(count_z), jnp.float32))

def smoothing_tables(columns, points_y):
    offsets = np.arange(3 * columns)[:, None] - columns - np.arange(columns)[None, :]
    sigma_x = columns / 2.0
    gauss_x = np.exp(-0.5 * (offsets / sigma_x) ** 2) * (np.abs(offsets) <= columns)
    normal_x = np.exp(-0.5 * (np.arange(-columns, columns + 1) / sigma_x) ** 2).sum()
    distance = np.arange(points_y)[:, None] - np.arange(points_y)[None, :]
    gauss_y = np.exp(-0.5 * (distance / SIGMA_Y) ** 2)
    gauss_y = gauss_y / gauss_y.sum(axis=1, keepdims=True)
    return (jnp.asarray(gauss_x / normal_x, jnp.float32), jnp.asarray(gauss_y, jnp.float32))

def make_coefs(kappa_grid, kappa_ext, tables):
    table_x, table_y, table_z, weight_x, weight_y, weight_z = tables
    coef_x = jnp.einsum('...p,np->...n', kappa_ext, table_x[1], precision=HIGHEST) * (weight_z[:, None, None] * weight_y[None, :, None] * table_x[2][None, None, :])
    coef_y = jnp.einsum('ny,...yx->...nx', table_y[1], kappa_grid, precision=HIGHEST) * (weight_z[:, None, None] * table_y[2][None, :, None] * weight_x[None, None, :])
    coef_z = jnp.einsum('nz,...zyx->...nyx', table_z[1], kappa_grid, precision=HIGHEST) * (table_z[2][:, None, None] * weight_y[None, :, None] * weight_x[None, None, :])
    return (coef_x, coef_y, coef_z)

def stiffness(wavefield, wavefield_ext, coefficients, tables):
    table_x, table_y, table_z = (tables[0], tables[1], tables[2])
    grad_x = jnp.einsum('...p,np->...n', wavefield_ext, table_x[0], precision=HIGHEST)
    part_x = jnp.einsum('...n,np->...p', coefficients[0] * grad_x, table_x[0], precision=HIGHEST)
    grad_y = jnp.einsum('ny,...yx->...nx', table_y[0], wavefield, precision=HIGHEST)
    part_y = jnp.einsum('ny,...nx->...yx', table_y[0], coefficients[1] * grad_y, precision=HIGHEST)
    grad_z = jnp.einsum('nz,...zyx->...nyx', table_z[0], wavefield, precision=HIGHEST)
    part_z = jnp.einsum('nz,...nyx->...zyx', table_z[0], coefficients[2] * grad_z, precision=HIGHEST)
    return (part_x, part_y + part_z)

def reference(adjoint_now, adjoint_prev, backward_now, backward_prev, kappa, density, edge_flip, receiver_index, adjoint_source):
    slices = N_CUTS
    columns = XL

    def to_slices(values):
        return jnp.moveaxis(values.reshape(values.shape[:-1] + (slices, columns)), -2, -4)

    def to_grid(values):
        moved = jnp.moveaxis(values, -4, -2)
        return moved.reshape(moved.shape[:-2] + (slices * columns,))
    flip_flags = edge_flip

    def reorient_slices(planes):
        return jnp.where(flip_flags[:, None, None, None] != 0, jnp.flip(planes, -2), planes)
    tables = build_tables(EX, EX, EY, EZ)
    kappa_cut = to_slices(kappa)
    mass_matrix = to_slices(density) * (tables[5][:, None, None] * tables[4][None, :, None] * tables[3][None, None, :])
    kappa_right = reorient_slices(jnp.roll(kappa_cut, -1, 0)[..., 0:1])
    coefficients = make_coefs(kappa_cut, jnp.concatenate([kappa_cut, kappa_right], -1), tables)
    receivers = receiver_index.reshape(slices, RECV)
    slice_rows = jnp.arange(slices)[:, None]

    def apply_stiffness(wavefield):
        right_plane = reorient_slices(jnp.roll(wavefield, -1, 0)[..., 0:1])
        part_x, part_yz = stiffness(wavefield, jnp.concatenate([wavefield, right_plane], -1), coefficients, tables)
        returned = jnp.roll(reorient_slices(part_x[..., columns:]), 1, 0)
        owned = jnp.concatenate([part_x[..., 0:1] + returned, part_x[..., 1:columns]], -1)
        return owned + part_yz

    def one_event(inputs):
        adj_now, adj_prev, back_now, back_prev, sources = inputs
        kernel = jnp.zeros_like(adj_now)
        for instant in range(STEPS):
            forcing = jnp.zeros((slices, ZP * YP * columns), jnp.float32).at[slice_rows, receivers].add(sources[instant].reshape(slices, RECV))
            accel_adj = (forcing.reshape(adj_now.shape) - apply_stiffness(adj_now)) / mass_matrix
            accel_back = (0.0 - apply_stiffness(back_now)) / mass_matrix
            kernel = kernel + DT2 * back_now * accel_adj
            adj_now, adj_prev = (2.0 * adj_now - adj_prev + DT2 * accel_adj, adj_now)
            back_now, back_prev = (2.0 * back_now - back_prev + DT2 * accel_back, back_now)
        return (adj_now, adj_prev, back_now, back_prev, kernel)
    results = lax.map(one_event, (to_slices(adjoint_now), to_slices(adjoint_prev), to_slices(backward_now), to_slices(backward_prev), adjoint_source))
    kernel_total = lax.optimization_barrier(jnp.sum(results[4], axis=0))
    table_x, table_y = smoothing_tables(columns, YP)
    left_part = jnp.roll(reorient_slices(kernel_total), 1, 0)
    right_part = reorient_slices(jnp.roll(kernel_total, -1, 0))
    extended = jnp.concatenate([left_part, kernel_total, right_part], -1)
    along_x = jnp.einsum('...j,ji->...i', extended, table_x, precision=HIGHEST)
    along_y = jnp.einsum('yv,...vx->...yx', table_y, along_x, precision=HIGHEST)
    return (to_grid(results[0]), to_grid(results[1]), to_grid(results[2]), to_grid(results[3]), to_grid(along_y))
```

```python
import functools

import jax
import jax.numpy as jnp
import numpy as np
from jax import lax
from jax.experimental import pallas as pl
from jax.experimental.pallas import tpu as pltpu
from jax.sharding import PartitionSpec as P

DT2 = 0.003
SIGMA_Y = 1.0
ZP, YP, XL = 17, 33, 128
YPAD = 40
ROWS = ZP * YPAD
HALF = 9
KROWS = 576
VMEM = 48 * 1024 * 1024


def gll_tables():
    nodes = np.array([-1.0, -np.sqrt(3.0 / 7.0), 0.0, np.sqrt(3.0 / 7.0), 1.0])
    weights = np.array([0.1, 49.0 / 90.0, 32.0 / 45.0, 49.0 / 90.0, 0.1])
    deriv = np.zeros((5, 5))
    for a in range(5):
        for b in range(5):
            for m in range(5):
                if m == b:
                    continue
                factor = 1.0 / (nodes[b] - nodes[m])
                for k in range(5):
                    if k == b or k == m:
                        continue
                    factor = factor * (nodes[a] - nodes[k]) / (nodes[b] - nodes[k])
                deriv[a, b] += factor
    return weights, deriv


GW, GD = gll_tables()
SHARED = np.array([0.2, GW[1], GW[2], GW[3], 0.2])
APPLY = GW[:, None] * GD
GATHER = (GD / SHARED[None, :]).T


def split(m):
    hi = np.asarray(m, np.float32).astype(jnp.bfloat16)
    lo = (np.asarray(m, np.float32) - hi.astype(np.float32)).astype(jnp.bfloat16)
    return jnp.asarray(hi), jnp.asarray(lo)


LANE_A, LANE_B, LANE_K, LANE_PA, LANE_CA, LANE_PB, LANE_CB = 0, 13, 26, 39, 44, 52, 57


def x_tables():
    def column(c):
        if 0 <= c < XL:
            return c
        return XL + (c + 8 if c < 0 else 8 + c - XL)

    def node(e, a):
        if 0 <= e < 32:
            return 4 * e + a if a < 4 else XL + e
        return XL + {-1: 32, -2: 37, 32: 42}[e] + a

    grad = np.zeros((2 * XL, 2 * XL))
    back = np.zeros((2 * XL, 2 * XL))
    pick = np.zeros((2 * XL, XL))
    for e in range(-2, 33):
        for a in range(5):
            n = node(e, a)
            for b in range(5):
                c = 4 * e + b
                grad[column(c), n] += APPLY[a, b]
                if -4 <= c <= XL:
                    back[n, column(c)] += GATHER[b, a]
            if n >= XL:
                k = column(4 * e + a)
                pick[k if k < XL else k + LANE_K, n - XL] = 1.0
    return split(grad), split(back), jnp.asarray(pick, jnp.bfloat16)


def smoothing_tables():
    offsets = np.arange(3 * XL)[:, None] - XL - np.arange(XL)[None, :]
    sigma_x = XL / 2.0
    gauss_x = np.exp(-0.5 * (offsets / sigma_x) ** 2) * (np.abs(offsets) <= XL)
    normal_x = np.exp(-0.5 * (np.arange(-XL, XL + 1) / sigma_x) ** 2).sum()
    distance = np.arange(YP)[:, None] - np.arange(YP)[None, :]
    gauss_y = np.exp(-0.5 * (distance / SIGMA_Y) ** 2)
    gauss_y = gauss_y / gauss_y.sum(axis=1, keepdims=True)
    undo = np.zeros((YP, YP))
    for y in range(YP):
        if y == 16:
            undo[y, y] = 1.0
        else:
            undo[y, 32 - y] = 0.5
            undo[y, y] = 0.5 if y < 16 else -0.5
    return gauss_x / normal_x, gauss_y @ undo


def apply5(m, x):
    e0, o0, e1, o1, mid = x[0] + x[4], x[0] - x[4], x[1] + x[3], x[1] - x[3], x[2]
    f = lambda v: np.float32(v)
    odd = [
        f((m[a, 0] + m[a, 4]) / 2) * e0 + f((m[a, 1] + m[a, 3]) / 2) * e1 + f(m[a, 2]) * mid
        for a in (0, 1)
    ]
    even = [
        f((m[a, 0] - m[a, 4]) / 2) * o0 + f((m[a, 1] - m[a, 3]) / 2) * o1 for a in (0, 1, 2)
    ]
    return [even[0] + odd[0], even[1] + odd[1], even[2], even[1] - odd[1], even[0] - odd[0]]


def apply_y(fields, kappa):
    row = lax.broadcasted_iota(jnp.int32, (8, XL), 0)

    def plane(z, carry):
        at = lambda a: pl.ds(a, 8, stride=4)
        k = [kappa[z, at(a), :] for a in range(5)]
        for v, out in fields:
            g = apply5(APPLY, [v[z, at(a), :] for a in range(5)])
            o = apply5(GATHER, [k[a] * g[a] for a in range(5)])
            moved = pltpu.roll(o[4], 1, 0)
            out[z, at(0), :] = jnp.where(row == 0, 2.0 * o[0], o[0] + moved)
            for b in range(1, 4):
                out[z, at(b), :] = o[b]
            out[z, 32:33, :] = 2.0 * moved[0:1]
        return carry

    lax.fori_loop(0, ZP, plane, 0)


def apply_z(fields, kappa, use):
    def block(rows):
        for i, v in enumerate(fields):
            ends = None
            for e in range(4):
                g = apply5(APPLY, [v[4 * e + a, rows, :] for a in range(5)])
                o = apply5(GATHER, [kappa[4 * e + a, rows, :] * g[a] for a in range(5)])
                use(i, 4 * e, rows, 2.0 * o[0] if e == 0 else o[0] + ends)
                for b in range(1, 4):
                    use(i, 4 * e + b, rows, o[b])
                ends = o[4]
            use(i, 16, rows, 2.0 * ends)

    def step(j, carry):
        block(pl.ds(pl.multiple_of(8 * j, 8), 8))
        return carry

    lax.fori_loop(0, 4, step, 0)
    block(pl.ds(32, 1))


def add_forcing(target, c_ref, index, source, instant, iz, iy):
    lane = lax.broadcasted_iota(jnp.int32, (1, XL), 1)
    node = lane % 4
    inv_x = jnp.where(
        node == 0, 1.0 / SHARED[0], jnp.where(node == 2, 1.0 / SHARED[2], 1.0 / SHARED[1])
    ).astype(jnp.float32)

    def one(r, carry):
        point = index[r]
        z = point // (YP * XL)
        rest = point - z * (YP * XL)
        y = rest // XL
        x = rest - y * XL
        amount = source[instant, r] * iz[z] * iy[y]
        at = (pl.ds(z, 1), pl.ds(y, 1), slice(None))
        change = jnp.where(lane == x, inv_x * amount, 0.0)
        target[at] = target[at] + c_ref[at] * change[None]
        return carry

    lax.fori_loop(0, 16, one, 0)


def flip_rows(source, target, flag):
    for y in range(YP):
        to = jnp.where(flag != 0, 32 - y, y)
        target[:, pl.ds(to, 1), :] = source[:, y : y + 1, :]


def pack_kernel(
    flip, index, source, iz, iy, an, ap, bn, bp, ka, de, c_out, f_out, right_out, left_out, pack
):
    lane = lax.broadcasted_iota(jnp.int32, (YP, XL), 1)
    f_out[...] = jnp.zeros_like(f_out)
    for z in range(ZP):
        c_out[z, 0:YP, :] = DT2 / de[z]
    add_forcing(f_out, c_out, index, source, 0, iz, iy)
    for z in range(ZP):
        group = 0 if z < HALF else 64
        a, b, k, c = an[0, z], bn[0, z], ka[z], c_out[z, 0:YP, :]
        pa = 2.0 * a - ap[0, z] + f_out[z, 0:YP, :]
        pb = 2.0 * b - bp[0, z]
        tile = None
        parts = [
            (a, 120, LANE_A), (b, 120, LANE_B), (k, 120, LANE_K), (pa, 124, LANE_PA),
            (c, 124, LANE_CA), (pb, 124, LANE_PB), (c, 124, LANE_CB),
        ]
        for value, first, to in reversed(parts):
            moved = pltpu.roll(value, (group + to - first) % XL, 1)
            if tile is None:
                tile = moved
            else:
                above = group + parts[[p[2] for p in parts].index(to) + 1][2]
                tile = jnp.where(lane < above, moved, tile)
        if group:
            pack[z - HALF, :, :] = jnp.where(lane < 64, pack[z - HALF, :, :], tile)
        else:
            pack[z, :, :] = tile
    left_out[...] = pack[...]
    flip_rows(pack, right_out, flip[0])


def local_kernel(index, source, iz, iy, an, bn, ka, c, f, a_out, b_out, f1_out):
    a, b = an.at[0], bn.at[0]
    apply_y(((a, a_out), (b, b_out)), ka)

    def use(i, z, rows, value):
        out = (a_out, b_out)[i]
        total = c[z, rows, :] * (out[z, rows, :] + value)
        out[z, rows, :] = f[z, rows, :] - total if i == 0 else -total

    apply_z((a, b), ka, use)
    f1_out[...] = jnp.zeros_like(f1_out)
    add_forcing(f1_out, c, index, source, 1, iz, iy)


def halves(x):
    hi = x.astype(jnp.bfloat16)
    return hi, (x - hi.astype(jnp.float32)).astype(jnp.bfloat16)


def dot(a, b):
    return jnp.dot(a, b, preferred_element_type=jnp.float32)


def dot3(x, m_hi, m_lo):
    hi, lo = halves(x)
    return dot(hi, m_hi) + dot(lo, m_hi) + dot(hi, m_lo)


def step_kernel(
    flip, an, ap, bn, bp, ka, c, a0, b0, f1, right_in, left_in,
    g_hi, g_lo, t_hi, t_lo, pick,
    af_out, al_out, bf_out, bl_out, k_out,
    left, u, ku, cu, qu, va, vb, kg, wa, wb, y1, y2,
):
    lane = lax.broadcasted_iota(jnp.int32, (YP, XL), 1)
    flip_rows(left_in, left, flip[0])
    before = None
    for first, n in (
        (LANE_A, 8), (LANE_B, 8), (LANE_K, 8), (LANE_PA, 4), (LANE_CA, 4), (LANE_PB, 4), (LANE_CB, 4)
    ):
        one = ((lane % 64) >= first) & ((lane % 64) < first + n)
        before = one if before is None else before | one
    for z in range(ZP):
        i = z % HALF
        tile = jnp.where(before, right_in[i], left[i])
        if z >= HALF:
            tile = pltpu.roll(tile, 64, 1)
        u[z, 0:YP, :] = tile
        ku[z, 0:YP, :] = jnp.where(
            lane < LANE_B,
            pltpu.roll(tile, XL - LANE_K, 1),
            pltpu.roll(tile, XL - LANE_K + LANE_B, 1),
        )
        qu[z, 0:YP, :] = pltpu.roll(tile, XL - LANE_PA + 4, 1)
        cu[z, 0:YP, :] = pltpu.roll(tile, XL - LANE_CA + 4, 1)
        va[z, 0:YP, :] = an[0, z]
        vb[z, 0:YP, :] = bn[0, z]
        kg[z, 0:YP, 0:XL] = ka[z]
    apply_y(((u, y1),), ku)

    def use(i, z, rows, value):
        qu[z, rows, :] = qu[z, rows, :] - cu[z, rows, :] * (y1[z, rows, :] + value)

    apply_z((u,), ku, use)

    flat = lambda ref: ref[...].reshape(ROWS, ref.shape[-1])
    tall = lambda value: value.reshape(ZP, YPAD, value.shape[-1])
    uf = flat(u)
    chosen = jnp.concatenate([kg[:, :, 0:XL].reshape(ROWS, XL), uf], 1)
    hi, lo = halves(chosen)
    kg[:, :, XL:] = tall(dot(hi, pick[...]) + dot(lo, pick[...]))

    def along_x(v, halo, wide):
        flux = dot3(jnp.concatenate([v, halo], 1), g_hi[...], g_lo[...]) * flat(kg)
        n = 2 * XL if wide else XL
        return dot3(flux, t_hi[:, 0:n], t_lo[:, 0:n])

    xa = along_x(flat(va), uf, True)
    xb = along_x(flat(vb), pltpu.roll(uf, XL - LANE_B, 1), True)
    lane2 = lax.broadcasted_iota(jnp.int32, (ROWS, XL), 1)
    halo = jnp.where(lane2 < LANE_B, xa[:, XL:], pltpu.roll(xb[:, XL:], LANE_B, 1))
    u1 = flat(qu) - flat(cu) * halo
    wa[...] = tall(xa[:, 0:XL])
    wb[...] = tall(xb[:, 0:XL])
    for z in range(ZP):
        cz = c[z, 0:YP, :]
        acc_a = a0[z, 0:YP, :] - cz * wa[z, 0:YP, :]
        acc_b = b0[z, 0:YP, :] - cz * wb[z, 0:YP, :]
        a, b = an[0, z], bn[0, z]
        v1a = 2.0 * a - ap[0, z] + acc_a
        v1b = 2.0 * b - bp[0, z] + acc_b
        al_out[0, z] = v1a
        bl_out[0, z] = v1b
        va[z, 0:YP, :] = v1a
        vb[z, 0:YP, :] = v1b
        ku[z, 0:YP, :] = b * acc_a
    apply_y(((va, y1), (vb, y2)), ka)

    def add(i, z, rows, value):
        out = (y1, y2)[i]
        out[z, rows, :] = out[z, rows, :] + value

    apply_z((va, vb), ka, add)
    xa = along_x(flat(va), u1, False)
    xb = along_x(flat(vb), pltpu.roll(u1, XL - LANE_B, 1), False)
    wa[...] = tall(xa)
    wb[...] = tall(xb)
    for z in range(ZP):
        cz = c[z, 0:YP, :]
        acc_a = f1[z, 0:YP, :] - cz * (wa[z, 0:YP, :] + y1[z, 0:YP, :])
        acc_b = -cz * (wb[z, 0:YP, :] + y2[z, 0:YP, :])
        v1a, v1b = va[z, 0:YP, :], vb[z, 0:YP, :]
        af_out[0, z] = 2.0 * v1a - an[0, z] + acc_a
        bf_out[0, z] = 2.0 * v1b - bn[0, z] + acc_b
        ku[z, 0:YP, :] = ku[z, 0:YP, :] + v1b * acc_a
    for y in range(YP):
        u[:, 32 - y : 33 - y, :] = ku[:, y : y + 1, :]
    row = lax.broadcasted_iota(jnp.int32, (YP, XL), 0)
    sign = jnp.where(row < 16, 1.0, jnp.where(row == 16, 0.0, -1.0)).astype(jnp.float32)
    k_out[ZP * 32 :, :] = jnp.zeros((KROWS - ZP * 32, XL), jnp.float32)
    for z in range(ZP):
        t = u[z, 0:YP, :] + sign * ku[z, 0:YP, :]
        k_out[32 * z : 32 * z + 32, :] = t[0:32]
        k_out[ZP * 32 + z : ZP * 32 + z + 1, :] = t[32:33]


def smooth_kernel(copies, before, own, after, gx_hi, gx_lo, out):
    total = None
    for i, part in enumerate((before, own, after)):
        at = slice(XL * i, XL * (i + 1))
        one = dot3(part[...], gx_hi[at, :], gx_lo[at, :])
        total = one if total is None else total + one
    for i in range(copies):
        out[i] = total


def finish_kernel(t, blocks_hi, blocks_lo, last, out):
    def planes(first, n):
        rows = t[32 * first : 32 * (first + n), :]
        hi, lo = halves(rows)
        m_hi, m_lo = blocks_hi[0 : n * YPAD, 0 : n * 32], blocks_lo[0 : n * YPAD, 0 : n * 32]
        done = dot(m_hi, hi) + dot(m_hi, lo) + dot(m_lo, hi)
        for i in range(n):
            z = first + i
            extra = last[...] * t[ZP * 32 + z : ZP * 32 + z + 1, :]
            out[z] = done[i * YPAD : i * YPAD + YP] + extra[0:YP]

    planes(0, 8)
    planes(8, 8)
    planes(16, 1)


SMEM_SPEC = pl.BlockSpec(memory_space=pltpu.SMEM)
VMEM_SPEC = pl.BlockSpec(memory_space=pltpu.VMEM)


def call(kernel, outs, scalars, arrays, scratch=(), flops=0, moved=0):
    return pl.pallas_call(
        kernel,
        out_shape=[jax.ShapeDtypeStruct(s, jnp.float32) for s in outs],
        in_specs=[SMEM_SPEC] * len(scalars) + [VMEM_SPEC] * len(arrays),
        out_specs=[VMEM_SPEC] * len(outs),
        scratch_shapes=[pltpu.VMEM(s, jnp.float32) for s in scratch],
        compiler_params=pltpu.CompilerParams(vmem_limit_bytes=VMEM),
        cost_estimate=pl.CostEstimate(flops=flops, bytes_accessed=moved, transcendentals=0),
    )(*scalars, *arrays)


def shift(value, axis, by):
    n = lax.axis_size(axis)
    return lax.ppermute(value, axis, [(i, (i + by) % n) for i in range(n)])


def local(an, ap, bn, bp, kappa, density, flip, index, source):
    field, padded, edge = (1, ZP, YP, XL), (ZP, YPAD, XL), (HALF, YP, XL)
    inv_z, inv_y = (np.tile(1.0 / SHARED[:4], n) for n in (4, 8))
    inv_z, inv_y = (np.append(v, v[0] * 2) for v in (inv_z, inv_y))
    inv_z[0] *= 2
    inv_y[0] *= 2
    iz, iy = jnp.asarray(inv_z, jnp.float32), jnp.asarray(inv_y, jnp.float32)
    src = source[0]
    c, f0, to_right, to_left = call(
        pack_kernel,
        [padded, padded, edge, edge],
        [flip, index, src, iz, iy],
        [an, ap, bn, bp, kappa, density],
        [edge],
        moved=3_000_000,
    )
    from_left = shift(to_right, "cuts", 1)
    from_right = shift(to_left, "cuts", -1)
    a0, b0, f1 = call(
        local_kernel,
        [padded, padded, padded],
        [index, src, iz, iy],
        [an, bn, kappa, c, f0],
        flops=20_000_000,
        moved=3_000_000,
    )
    (g_hi, g_lo), (t_hi, t_lo), pick = x_tables()
    wide = (ZP, YPAD, 2 * XL)
    af, al, bf, bl, k = call(
        step_kernel,
        [field, field, field, field, (KROWS, XL)],
        [flip],
        [an, ap, bn, bp, kappa, c, a0, b0, f1, from_left, from_right, g_hi, g_lo, t_hi, t_lo, pick],
        [edge, padded, padded, padded, padded, padded, padded, wide, padded, padded, padded, padded],
        flops=600_000_000,
        moved=6_000_000,
    )
    groups = lax.axis_size("event")
    part = KROWS // groups
    parts = lax.all_to_all(k.reshape(groups, part, XL), "event", 0, 0)
    total = jnp.sum(parts, axis=0)
    row = lax.axis_index("event") * part + jnp.arange(part)
    odd = jnp.where(row < ZP * 32, row % 32 > 16, True)
    sign = jnp.where(odd & (flip[0] != 0), -1.0, 1.0).astype(jnp.float32)[:, None]
    before = shift(total * sign, "cuts", 1)
    after = shift(total, "cuts", -1) * sign
    gauss_x, final_y = smoothing_tables()
    spread = call(
        functools.partial(smooth_kernel, groups),
        [(groups, part, XL)],
        [],
        [before, total, after, *split(gauss_x)],
    )[0]
    whole = lax.all_to_all(spread, "event", 0, 0).reshape(KROWS, XL)
    blocks = np.zeros((8 * YPAD, 256))
    for i in range(8):
        blocks[i * YPAD : i * YPAD + YP, i * 32 : i * 32 + 32] = final_y[:, 0:32]
    last = np.zeros((YPAD, XL))
    last[0:YP] = final_y[:, 32:33]
    smoothed = call(
        finish_kernel, [(ZP, YP, XL)], [], [whole, *split(blocks), jnp.asarray(last, jnp.float32)]
    )[0]
    return af, al, bf, bl, smoothed


def solution(mesh):
    field = P("event", None, None, "cuts")
    grid = P(None, None, "cuts")
    return jax.shard_map(
        local,
        mesh=mesh,
        in_specs=(field,) * 4 + (grid, grid, P("cuts"), P("cuts"), P("event", None, "cuts")),
        out_specs=(field,) * 4 + (grid,),
        check_vma=False,
    )
```

```python
import jax
import jax.numpy as jnp
import numpy as np
from jax import lax
from jax.experimental import pallas as pl
from jax.experimental.pallas import tpu as pltpu
from jax.sharding import PartitionSpec as P

DT2 = 0.003
SIGMA_Y = 1.0
ZP, YP, XL = 17, 33, 128
YPAD = 40
ROWS = ZP * YPAD
HALF = 9
KROWS = 576


def gll_tables():
    nodes = np.array([-1.0, -np.sqrt(3.0 / 7.0), 0.0, np.sqrt(3.0 / 7.0), 1.0])
    weights = np.array([0.1, 49.0 / 90.0, 32.0 / 45.0, 49.0 / 90.0, 0.1])
    deriv = np.zeros((5, 5))
    for a in range(5):
        for b in range(5):
            for m in range(5):
                if m == b:
                    continue
                factor = 1.0 / (nodes[b] - nodes[m])
                for k in range(5):
                    if k == b or k == m:
                        continue
                    factor = factor * (nodes[a] - nodes[k]) / (nodes[b] - nodes[k])
                deriv[a, b] += factor
    return weights, deriv


GW, GD = gll_tables()
SHARED = np.array([0.2, GW[1], GW[2], GW[3], 0.2])
APPLY = GW[:, None] * GD
GATHER = (GD / SHARED[None, :]).T


def split(m):
    hi = np.asarray(m, np.float32).astype(jnp.bfloat16)
    lo = (np.asarray(m, np.float32) - hi.astype(np.float32)).astype(jnp.bfloat16)
    return hi, lo


LANE_A, LANE_B, LANE_K, LANE_PA, LANE_CA, LANE_PB, LANE_CB = 0, 13, 26, 39, 44, 52, 57


def x_tables():
    def node(e, a):
        if 0 <= e < 32:
            return 4 * e + a if a < 4 else XL + e
        return XL + {-1: 32, -2: 37, 32: 42}[e] + a

    def halo(c):
        return c + 8 if c < 0 else 8 + c - XL

    grad, edge = np.zeros((XL, 2 * XL)), np.zeros((XL, 2 * XL))
    back = np.zeros((2 * XL, 2 * XL))
    pick, pick_edge = np.zeros((XL, XL)), np.zeros((XL, XL))
    for e in range(-2, 33):
        for a in range(5):
            n = node(e, a)
            for b in range(5):
                c = 4 * e + b
                own = 0 <= c < XL
                (grad if own else edge)[c if own else halo(c), n] += APPLY[a, b]
                if -4 <= c <= XL:
                    back[n, c if own else XL + halo(c)] += GATHER[b, a]
            if n >= XL:
                c = 4 * e + a
                if 0 <= c < XL:
                    pick[c, n - XL] = 1.0
                else:
                    pick_edge[LANE_K + halo(c), n - XL] = 1.0
    return grad, edge, back, pick, pick_edge


def tables():
    grad, edge, back, pick, pick_edge = x_tables()
    g_hi, g_lo = split(grad)
    e_hi, e_lo = split(edge)
    first = np.zeros((2 * XL, 5 * XL), jnp.bfloat16)
    for i, (part, choose) in enumerate(((e_hi, 1.0), (e_hi, 1.0), (e_lo, 0.0))):
        rows = np.asarray(part)
        first[64 * i : 64 * i + 13, 0 : 2 * XL] = rows[0:13]
        first[64 * i + LANE_B : 64 * i + LANE_B + 13, 2 * XL : 4 * XL] = rows[0:13]
        first[64 * i : 64 * i + 64, 4 * XL :] = (choose * pick_edge[0:64]).astype(jnp.bfloat16)
    second = []
    for at in (LANE_A, LANE_B):
        m = np.zeros((XL, 2 * XL), jnp.bfloat16)
        for i, part in enumerate((e_hi, e_hi, e_lo)):
            m[32 * i + at + 4 : 32 * i + at + 9] = np.asarray(part)[4:9]
        second.append(np.concatenate([np.asarray(g_lo), m], 0))
    t_hi, t_lo = (np.asarray(t) for t in split(back))
    moved = [np.roll(t[:, XL:], LANE_B, 1) for t in (t_hi, t_lo)]
    return dict(
        grad=np.concatenate([np.asarray(g_hi)] * 2, 0),
        grad_lo=np.asarray(g_lo),
        pick=np.concatenate([pick, pick], 0).astype(jnp.bfloat16),
        first=first,
        second_a=second[0],
        second_b=second[1],
        ta_hi=t_hi,
        ta_lo=t_lo,
        tb_hi=np.concatenate([t_hi[:, :XL], moved[0]], 1),
        tb_lo=np.concatenate([t_lo[:, :XL], moved[1]], 1),
        t_both=np.concatenate([t_hi[:, :XL], t_lo[:, :XL]], 1),
    )


def smoothing_tables():
    offsets = np.arange(3 * XL)[:, None] - XL - np.arange(XL)[None, :]
    sigma_x = XL / 2.0
    gauss_x = np.exp(-0.5 * (offsets / sigma_x) ** 2) * (np.abs(offsets) <= XL)
    normal_x = np.exp(-0.5 * (np.arange(-XL, XL + 1) / sigma_x) ** 2).sum()
    distance = np.arange(YP)[:, None] - np.arange(YP)[None, :]
    gauss_y = np.exp(-0.5 * (distance / SIGMA_Y) ** 2)
    gauss_y = gauss_y / gauss_y.sum(axis=1, keepdims=True)
    undo = np.zeros((YP, YP))
    for y in range(YP):
        if y == 16:
            undo[y, y] = 1.0
        else:
            undo[y, 32 - y] = 0.5
            undo[y, y] = 0.5 if y < 16 else -0.5
    return gauss_x / normal_x, gauss_y @ undo


def apply5(m, x):
    e0, o0, e1, o1, mid = x[0] + x[4], x[0] - x[4], x[1] + x[3], x[1] - x[3], x[2]
    f = lambda v: np.float32(v)
    odd = [
        f((m[a, 0] + m[a, 4]) / 2) * e0 + f((m[a, 1] + m[a, 3]) / 2) * e1 + f(m[a, 2]) * mid
        for a in (0, 1)
    ]
    even = [
        f((m[a, 0] - m[a, 4]) / 2) * o0 + f((m[a, 1] - m[a, 3]) / 2) * o1 for a in (0, 1, 2)
    ]
    return [even[0] + odd[0], even[1] + odd[1], even[2], even[1] - odd[1], even[0] - odd[0]]


def apply_y(fields, kappa):
    row = lax.broadcasted_iota(jnp.int32, (8, XL), 0)

    def plane(z, carry):
        at = lambda a: pl.ds(a, 8, stride=4)
        k = [kappa[z, at(a), :] for a in range(5)]
        for v, out in fields:
            g = apply5(APPLY, [v[z, at(a), :] for a in range(5)])
            o = apply5(GATHER, [k[a] * g[a] for a in range(5)])
            moved = pltpu.roll(o[4], 1, 0)
            out[z, at(0), :] = jnp.where(row == 0, 2.0 * o[0], o[0] + moved)
            for b in range(1, 4):
                out[z, at(b), :] = o[b]
            out[z, 32:33, :] = 2.0 * moved[0:1]
        return carry

    lax.fori_loop(0, ZP, plane, 0)


def apply_z(fields, kappa, use):
    def block(rows):
        for i, v in enumerate(fields):
            ends = None
            for e in range(4):
                g = apply5(APPLY, [v[4 * e + a, rows, :] for a in range(5)])
                o = apply5(GATHER, [kappa[4 * e + a, rows, :] * g[a] for a in range(5)])
                use(i, 4 * e, rows, 2.0 * o[0] if e == 0 else o[0] + ends)
                for b in range(1, 4):
                    use(i, 4 * e + b, rows, o[b])
                ends = o[4]
            use(i, 16, rows, 2.0 * ends)

    def step(j, carry):
        block(pl.ds(pl.multiple_of(8 * j, 8), 8))
        return carry

    lax.fori_loop(0, 4, step, 0)
    block(pl.ds(32, 1))


def add_forcing(target, c_ref, index, source, instant, iz, iy):
    lane = lax.broadcasted_iota(jnp.int32, (1, XL), 1)
    node = lane % 4
    inv_x = jnp.where(
        node == 0, 1.0 / SHARED[0], jnp.where(node == 2, 1.0 / SHARED[2], 1.0 / SHARED[1])
    ).astype(jnp.float32)
    for r in range(16):
        point = index[r]
        row = lax.shift_right_logical(point, 7)
        z = lax.shift_right_logical(row * 1986, 16)
        y = row - z * YP
        amount = source[instant, r] * iz[z] * iy[y]
        at = (pl.ds(z, 1), pl.ds(y, 1), slice(None))
        change = jnp.where(lane == (point & (XL - 1)), inv_x * amount, 0.0)
        target[at] = target[at] + c_ref[at] * change[None]


def flip_rows(source, target, flag):
    for y in range(YP):
        to = jnp.where(flag != 0, 32 - y, y)
        target[:, pl.ds(to, 1), :] = source[:, y : y + 1, :]


def pack_kernel(
    flip, index, source, iz, iy, an_in, bn_in, ap_in, bp_in, ka_in, de_in,
    right_out, left_out, an, bn, ap, bp, ka, c_out, f_out, pack, de, sem,
):
    rows = slice(0, YP)
    copies = [
        pltpu.make_async_copy(de_in, de.at[:, rows, :], sem.at[0]),
        pltpu.make_async_copy(ka_in, ka.at[:, rows, :], sem.at[1]),
    ]
    for i, (src, dst) in enumerate(((an_in, an), (bn_in, bn), (ap_in, ap), (bp_in, bp))):
        copies.append(pltpu.make_async_copy(src.at[:, :, 0, :], dst.at[:, rows, :], sem.at[2 + i]))
    for copy in copies:
        copy.start()
    f_out[...] = jnp.zeros_like(f_out)
    lane = lax.broadcasted_iota(jnp.int32, (YP, XL), 1)
    copies[0].wait()
    for z in range(ZP):
        c_out[z, 0:YP, :] = DT2 / de[z, 0:YP, :]
    add_forcing(f_out, c_out, index, source, 0, iz, iy)
    for copy in copies[1:]:
        copy.wait()
    for z in range(ZP):
        group = 0 if z < HALF else 64
        a, b, k, c = an[z, rows, :], bn[z, rows, :], ka[z, rows, :], c_out[z, rows, :]
        pa = 2.0 * a - ap[z, rows, :] + f_out[z, rows, :]
        pb = 2.0 * b - bp[z, rows, :]
        tile = None
        parts = [
            (a, 120, LANE_A), (b, 120, LANE_B), (k, 120, LANE_K), (pa, 124, LANE_PA),
            (c, 124, LANE_CA), (pb, 124, LANE_PB), (c, 124, LANE_CB),
        ]
        above = None
        for value, first, to in reversed(parts):
            moved = pltpu.roll(value, (group + to - first) % XL, 1)
            tile = moved if tile is None else jnp.where(lane < above, moved, tile)
            above = group + to
        if group:
            pack[z - HALF, :, :] = jnp.where(lane < 64, pack[z - HALF, :, :], tile)
        else:
            pack[z, :, :] = tile
    left_out[...] = pack[...]
    flip_rows(pack, right_out, flip[0])


def dot(a, b):
    return jnp.dot(a, b, preferred_element_type=jnp.float32)


def halves(x):
    hi = x.astype(jnp.bfloat16)
    return hi, (x - hi.astype(jnp.float32)).astype(jnp.bfloat16)


def dot3(x, m_hi, m_lo):
    hi, lo = halves(x)
    return dot(hi, m_hi) + dot(lo, m_hi) + dot(hi, m_lo)


def flat(ref):
    return ref[...].reshape(ROWS, ref.shape[-1])


def local_kernel(
    index, source, iz, iy, a, b, ka, c, f, grad, grad_lo, pick,
    a_out, b_out, f1_out, ga_out, gb_out, kg_out,
):
    apply_y(((a, a_out), (b, b_out)), ka)

    def use(i, z, rows, value):
        out = (a_out, b_out)[i]
        total = c[z, rows, :] * (out[z, rows, :] + value)
        out[z, rows, :] = f[z, rows, :] - total if i == 0 else -total

    apply_z((a, b), ka, use)
    f1_out[...] = jnp.zeros_like(f1_out)
    add_forcing(f1_out, c, index, source, 1, iz, iy)
    for field, out in ((a, ga_out), (b, gb_out)):
        hi, lo = halves(flat(field))
        out[...] = dot(jnp.concatenate([hi, lo], 1), grad[...]) + dot(hi, grad_lo[...])
    hi, lo = halves(flat(ka))
    kg_out[...] = dot(jnp.concatenate([hi, lo], 1), pick[...])


def step_kernel(
    flip, an, ap, bn, bp, ka, c, a0, b0, f1, ga, gb, kg0, right_in, left_in,
    first, grad, second_a, ta_hi, ta_lo, tb_hi, tb_lo, t_both,
    k_out, al_out, bl_out, af_out, v1b, u1_out, kg,
    left, u, ku, cu, qu, wa, wb, y1, v1a, k, sem,
):
    lane = lax.broadcasted_iota(jnp.int32, (YP, XL), 1)
    rows = slice(0, YP)
    sent = []

    def send(src, dst, dense):
        if dense:
            src, dst = src.at[:, rows, :], dst.at[:, :, 0, :]
        sent.append(pltpu.make_async_copy(src, dst, sem.at[len(sent)]))
        sent[-1].start()

    flip_rows(left_in, left, flip[0])
    before = None
    for start, n in (
        (LANE_A, 8), (LANE_B, 8), (LANE_K, 8), (LANE_PA, 4), (LANE_CA, 4), (LANE_PB, 4), (LANE_CB, 4)
    ):
        one = ((lane % 64) >= start) & ((lane % 64) < start + n)
        before = one if before is None else before | one
    for z in range(ZP):
        i = z % HALF
        tile = jnp.where(before, right_in[i], left[i])
        if z >= HALF:
            tile = pltpu.roll(tile, 64, 1)
        u[z, rows, :] = tile
        ku[z, rows, :] = jnp.where(
            lane < LANE_B,
            pltpu.roll(tile, XL - LANE_K, 1),
            pltpu.roll(tile, XL - LANE_K + LANE_B, 1),
        )
        qu[z, rows, :] = pltpu.roll(tile, XL - LANE_PA + 4, 1)
        cu[z, rows, :] = pltpu.roll(tile, XL - LANE_CA + 4, 1)
    apply_y(((u, y1),), ku)

    def use(i, z, rows, value):
        qu[z, rows, :] = qu[z, rows, :] - cu[z, rows, :] * (y1[z, rows, :] + value)

    apply_z((u,), ku, use)

    lane2 = lax.broadcasted_iota(jnp.int32, (ROWS, XL), 1)
    tall = lambda value: value.reshape(ZP, YPAD, value.shape[-1])
    hi, lo = halves(flat(u))
    low = pltpu.roll(lo.astype(jnp.float32), 64, 1)
    mixed = jnp.where(lane2 < 64, hi.astype(jnp.float32), low).astype(jnp.bfloat16)
    edge = dot(jnp.concatenate([mixed, hi], 1), first[...])
    kg[...] = jnp.concatenate([flat(ka), kg0[...] + edge[:, 4 * XL :]], 1)
    xa = dot3((ga[...] + edge[:, 0 : 2 * XL]) * kg[...], ta_hi[...], ta_lo[...])
    xb = dot3((gb[...] + edge[:, 2 * XL : 4 * XL]) * kg[...], tb_hi[...], tb_lo[...])
    u1 = flat(qu) - flat(cu) * (xa[:, XL:] + xb[:, XL:])
    hi = u1.astype(jnp.bfloat16).astype(jnp.float32)
    packed = jnp.where(
        lane2 < 32,
        hi,
        jnp.where(lane2 < 64, pltpu.roll(u1 - hi, 32, 1), pltpu.roll(hi, 64, 1)),
    ).astype(jnp.bfloat16)
    u1_out[...] = packed
    wa[...] = tall(xa[:, 0:XL])
    wb[...] = tall(xb[:, 0:XL])
    for z in range(ZP):
        cz = c[z, rows, :]
        acc_a = a0[z, rows, :] - cz * wa[z, rows, :]
        acc_b = b0[z, rows, :] - cz * wb[z, rows, :]
        a, b = an[z, rows, :], bn[z, rows, :]
        v1a[z, rows, :] = 2.0 * a - ap[z, rows, :] + acc_a
        v1b[z, rows, :] = 2.0 * b - bp[z, rows, :] + acc_b
        ku[z, rows, :] = b * acc_a
    send(v1a, al_out, True)
    send(v1b, bl_out, True)
    apply_y(((v1a, y1),), ka)

    def add(i, z, rows, value):
        y1[z, rows, :] = y1[z, rows, :] + value

    apply_z((v1a,), ka, add)
    wa[...] = tall(second_x(v1a, packed, grad, second_a, kg, t_both))
    for z in range(ZP):
        acc_a = f1[z, rows, :] - c[z, rows, :] * (wa[z, rows, :] + y1[z, rows, :])
        ku[z, rows, :] = ku[z, rows, :] + v1b[z, rows, :] * acc_a
        wb[z, rows, :] = 2.0 * v1a[z, rows, :] - an[z, rows, :] + acc_a
    send(wb, af_out, True)
    for y in range(YP):
        u[:, 32 - y : 33 - y, :] = ku[:, y : y + 1, :]
    row = lax.broadcasted_iota(jnp.int32, (YP, XL), 0)
    sign = jnp.where(row < 16, 1.0, jnp.where(row == 16, 0.0, -1.0)).astype(jnp.float32)
    k[ZP * 32 :, :] = jnp.zeros((KROWS - ZP * 32, XL), jnp.float32)
    for z in range(ZP):
        t = u[z, rows, :] + sign * ku[z, rows, :]
        k[32 * z : 32 * z + 32, :] = t[0:32]
        k[ZP * 32 + z : ZP * 32 + z + 1, :] = t[32:33]
        if z in (4, 8, 12):
            at = pl.ds(32 * (z - 4), 128)
            send(k.at[at], k_out.at[at], False)
    at = pl.ds(384, KROWS - 384)
    send(k.at[at], k_out.at[at], False)
    for copy in sent:
        copy.wait()


def second_x(v, packed, grad, second, kg, t_both):
    hi, lo = halves(flat(v))
    g = dot(jnp.concatenate([hi, lo], 1), grad[...])
    g = g + dot(jnp.concatenate([hi, packed], 1), second[...])
    hi, lo = halves(g * kg[...])
    both = dot(hi, t_both[...])
    return both[:, 0:XL] + both[:, XL:] + dot(lo, t_both[:, 0:XL])


def last_kernel(bn, ka, c, v1b, u1, kg, grad, second_b, t_both, bf_out, y1, wb, sem):
    rows = slice(0, YP)
    apply_y(((v1b, y1),), ka)

    def add(i, z, rows, value):
        y1[z, rows, :] = y1[z, rows, :] + value

    apply_z((v1b,), ka, add)
    x = second_x(v1b, u1[...], grad, second_b, kg, t_both)
    wb[...] = x.reshape(ZP, YPAD, XL)
    for z in range(ZP):
        acc = c[z, rows, :] * (wb[z, rows, :] + y1[z, rows, :])
        wb[z, rows, :] = 2.0 * v1b[z, rows, :] - bn[z, rows, :] - acc
    copy = pltpu.make_async_copy(wb.at[:, rows, :], bf_out.at[:, :, 0, :], sem.at[0])
    copy.start()
    copy.wait()


def odd_sign(flip, group, part):
    row = group[0] * part + lax.broadcasted_iota(jnp.int32, (part, XL), 0)
    odd = ((row & 31) > 16) | (row >= ZP * 32)
    return jnp.where(odd & (flip[0] != 0), -1.0, 1.0).astype(jnp.float32)


def sum_kernel(flip, group, parts, total_out, signed_out):
    total = parts[0]
    for i in range(1, parts.shape[0]):
        total = total + parts[i]
    total_out[...] = total
    signed_out[...] = total * odd_sign(flip, group, total.shape[0])


def smooth_kernel(flip, group, before, own, after, gx_hi, gx_lo, out, done, sem):
    sign = odd_sign(flip, group, own.shape[0])
    total = None
    for i, part in enumerate((before[...], own[...], after[...] * sign)):
        at = slice(XL * i, XL * (i + 1))
        one = dot3(part, gx_hi[at, :], gx_lo[at, :])
        total = one if total is None else total + one
    done[...] = total
    copies = [pltpu.make_async_copy(done, out.at[i], sem.at[i]) for i in range(out.shape[0])]
    for copy in copies:
        copy.start()
    for copy in copies:
        copy.wait()


def finish_kernel(t, blocks_hi, blocks_lo, last, out, done_all, sem):
    def planes(first, n):
        rows = t[32 * first : 32 * (first + n), :]
        hi, lo = halves(rows)
        m_hi, m_lo = blocks_hi[0 : n * YPAD, 0 : n * 32], blocks_lo[0 : n * YPAD, 0 : n * 32]
        done = dot(m_hi, hi) + dot(m_hi, lo) + dot(m_lo, hi)
        for i in range(n):
            z = first + i
            extra = last[...] * t[ZP * 32 + z : ZP * 32 + z + 1, :]
            done_all[z] = done[i * YPAD : (i + 1) * YPAD] + extra
        at = pl.ds(first, n)
        copy = pltpu.make_async_copy(done_all.at[at, 0:YP, :], out.at[at], sem.at[first // 8])
        copy.start()
        return copy

    for copy in [planes(0, 8), planes(8, 8), planes(16, 1)]:
        copy.wait()


SMEM_SPEC = pl.BlockSpec(memory_space=pltpu.SMEM)
VMEM_SPEC = pl.BlockSpec(memory_space=pltpu.VMEM)
ANY_SPEC = pl.BlockSpec(memory_space=pl.ANY)


def near(*shape, dtype=jnp.float32):
    return pltpu.VMEM(shape, dtype)


def far(*shape, dtype=jnp.float32):
    return pltpu.HBM(shape, dtype)


def call(kernel, outs, scalars, arrays, scratch=(), far_in=False, flops=0, moved=0, limit=24):
    if far_in:
        arrays = [pltpu.with_memory_space_constraint(v, pltpu.HBM) for v in arrays]
    out_specs = [ANY_SPEC if o.memory_space == pltpu.HBM else VMEM_SPEC for o in outs]
    return pl.pallas_call(
        kernel,
        out_shape=outs,
        in_specs=[SMEM_SPEC] * len(scalars) + [ANY_SPEC if far_in else VMEM_SPEC] * len(arrays),
        out_specs=out_specs,
        scratch_shapes=list(scratch),
        compiler_params=pltpu.CompilerParams(vmem_limit_bytes=limit * 1024 * 1024),
        cost_estimate=pl.CostEstimate(flops=flops, bytes_accessed=moved, transcendentals=0),
    )(*scalars, *arrays)


def shift(value, axis, by):
    n = lax.axis_size(axis)
    return lax.ppermute(value, axis, [(i, (i + by) % n) for i in range(n)])


def local(an, ap, bn, bp, kappa, density, flip, index, source):
    dense, padded, edge = far(ZP, YP, 1, XL), near(ZP, YPAD, XL), near(HALF, YP, XL)
    inv_z, inv_y = (np.tile(1.0 / SHARED[:4], n) for n in (4, 8))
    inv_z, inv_y = (np.append(v, v[0] * 2) for v in (inv_z, inv_y))
    inv_z[0] *= 2
    inv_y[0] *= 2
    iz, iy = jnp.asarray(inv_z, jnp.float32), jnp.asarray(inv_y, jnp.float32)
    src = source[0]
    tab = {name: jnp.asarray(value) for name, value in tables().items()}
    fields = [v.reshape(ZP, YP, 1, XL) for v in (an, bn, ap, bp)]
    dma = pltpu.SemaphoreType.DMA
    to_right, to_left, an, bn, ap, bp, ka, c, f0 = call(
        pack_kernel,
        [edge, edge] + [padded] * 7,
        [flip, index, src, iz, iy],
        [*fields, kappa, density],
        [edge, padded, dma((6,))],
        far_in=True,
        moved=4_000_000,
    )
    from_left = shift(to_right, "cuts", 1)
    from_right = shift(to_left, "cuts", -1)
    wide, narrow = near(ROWS, 2 * XL), near(ROWS, XL)
    a0, b0, f1, ga, gb, kg0 = call(
        local_kernel,
        [padded, padded, padded, wide, wide, narrow],
        [index, src, iz, iy],
        [an, bn, ka, c, f0, tab["grad"], tab["grad_lo"], tab["pick"]],
        flops=300_000_000,
        moved=5_000_000,
    )
    packed = near(ROWS, XL, dtype=jnp.bfloat16)
    k, al, bl, af, v1b, u1, kg = call(
        step_kernel,
        [far(KROWS, XL), dense, dense, dense, padded, packed, wide],
        [flip],
        [an, ap, bn, bp, ka, c, a0, b0, f1, ga, gb, kg0, from_left, from_right]
        + [tab[n] for n in ("first", "grad", "second_a", "ta_hi", "ta_lo", "tb_hi", "tb_lo", "t_both")],
        [edge] + [padded] * 8 + [near(KROWS, XL), dma((7,))],
        flops=600_000_000,
        moved=6_000_000,
    )
    groups = lax.axis_size("event")
    part = KROWS // groups
    parts = lax.all_to_all(k.reshape(groups, part, XL), "event", 0, 0)
    bf = call(
        last_kernel,
        [dense],
        [],
        [bn, ka, c, v1b, u1, kg, tab["grad"], tab["second_b"], tab["t_both"]],
        [padded, padded, dma((1,))],
        flops=300_000_000,
        moved=5_000_000,
    )[0]
    outs = (af, al, bf, bl)
    group = lax.axis_index("event").astype(jnp.int32).reshape(1)
    total, signed = call(sum_kernel, [near(part, XL)] * 2, [flip, group], [parts])
    before = shift(signed, "cuts", 1)
    after = shift(total, "cuts", -1)
    gauss_x, final_y = smoothing_tables()
    spread = call(
        smooth_kernel,
        [far(groups, part, XL)],
        [flip, group],
        [before, total, after, *(jnp.asarray(v) for v in split(gauss_x))],
        [near(part, XL), dma((8,))],
    )[0]
    whole = lax.all_to_all(spread, "event", 0, 0).reshape(KROWS, XL)
    blocks = np.zeros((8 * YPAD, 256))
    for i in range(8):
        blocks[i * YPAD : i * YPAD + YP, i * 32 : i * 32 + 32] = final_y[:, 0:32]
    last = np.zeros((YPAD, XL))
    last[0:YP] = final_y[:, 32:33]
    smoothed = call(
        finish_kernel,
        [far(ZP, YP, XL)],
        [],
        [whole, *(jnp.asarray(v) for v in split(blocks)), jnp.asarray(last, jnp.float32)],
        [near(ZP, YPAD, XL), dma((3,))],
    )[0]
    return *(v.reshape(1, ZP, YP, XL) for v in outs), smoothed


def solution(mesh):
    field = P("event", None, None, "cuts")
    grid = P(None, None, "cuts")
    return jax.shard_map(
        local,
        mesh=mesh,
        in_specs=(field,) * 4 + (grid, grid, P("cuts"), P("cuts"), P("event", None, "cuts")),
        out_specs=(field,) * 4 + (grid,),
        check_vma=False,
    )
```

```python
import jax
import jax.numpy as jnp
import numpy as np
from jax import lax
from jax.experimental import pallas as pl
from jax.experimental.pallas import tpu as pltpu
from jax.sharding import PartitionSpec as P

DT2 = 0.003
SIGMA_Y = 1.0
ZP, YP, XL = 17, 33, 128
YPAD = 40
ROWS = ZP * YPAD
PLANES, GROUP = 6, 42
KROWS = 576
UNROLL_Y, UNROLL_Z = 17, 4


def gll_tables():
    nodes = np.array([-1.0, -np.sqrt(3.0 / 7.0), 0.0, np.sqrt(3.0 / 7.0), 1.0])
    weights = np.array([0.1, 49.0 / 90.0, 32.0 / 45.0, 49.0 / 90.0, 0.1])
    deriv = np.zeros((5, 5))
    for a in range(5):
        for b in range(5):
            for m in range(5):
                if m == b:
                    continue
                factor = 1.0 / (nodes[b] - nodes[m])
                for k in range(5):
                    if k == b or k == m:
                        continue
                    factor = factor * (nodes[a] - nodes[k]) / (nodes[b] - nodes[k])
                deriv[a, b] += factor
    return weights, deriv


GW, GD = gll_tables()
SHARED = np.array([0.2, GW[1], GW[2], GW[3], 0.2])
APPLY = GW[:, None] * GD
GATHER = (GD / SHARED[None, :]).T


def split(m):
    hi = np.asarray(m, np.float32).astype(jnp.bfloat16)
    lo = (np.asarray(m, np.float32) - hi.astype(np.float32)).astype(jnp.bfloat16)
    return hi, lo


LANE_B, LANE_K, LANE_PA, LANE_CA, LANE_PB, LANE_CB = 8, 16, 21, 25, 29, 33
AFTER = 64


def x_tables():
    def node(e, a):
        if 0 <= e < 32:
            return 4 * e + a if a < 4 else XL + e
        return XL + {-1: 32, -2: 37, 32: 42}[e] + a

    def halo(c):
        return c + 8 if c < 0 else AFTER + c - XL

    grad, edge = np.zeros((XL, 2 * XL)), np.zeros((XL, 2 * XL))
    back = np.zeros((2 * XL, 2 * XL))
    pick, pick_edge = np.zeros((XL, XL)), np.zeros((XL, XL))
    for e in range(-2, 33):
        for a in range(5):
            n = node(e, a)
            for b in range(5):
                c = 4 * e + b
                own = 0 <= c < XL
                (grad if own else edge)[c if own else halo(c), n] += APPLY[a, b]
                if -4 <= c <= XL:
                    back[n, c if own else XL + halo(c)] += GATHER[b, a]
            if n >= XL:
                c = 4 * e + a
                if 0 <= c < XL:
                    pick[c, n - XL] = 1.0
                else:
                    pick_edge[LANE_K + halo(c), n - XL] = 1.0
    return grad, edge, back, pick, pick_edge


def tables():
    grad, edge, back, pick, pick_edge = x_tables()
    g_hi, g_lo = split(grad)
    e_hi, e_lo = split(edge)
    high, low = np.zeros((XL, 5 * XL), jnp.bfloat16), np.zeros((XL, 5 * XL), jnp.bfloat16)
    for m, part in ((high, e_hi), (low, e_lo)):
        m[:, 0 : 2 * XL] = part
        m[:, 2 * XL : 4 * XL] = np.roll(part, LANE_B, 0)
    high[:, 4 * XL :] = pick_edge.astype(jnp.bfloat16)
    second = []
    for at in (0, LANE_B):
        m = np.zeros((XL, 2 * XL), jnp.bfloat16)
        for i, part in enumerate((e_hi, e_hi, e_lo)):
            for lane in (4, 5, 6, 7, AFTER):
                m[16 * i + at + lane] = part[lane]
        second.append(np.concatenate([g_lo, m], 0))
    t_hi, t_lo = split(back)
    moved = [np.roll(t[:, XL:], LANE_B, 1) for t in (t_hi, t_lo)]
    return dict(
        grad=np.concatenate([g_hi] * 2, 0),
        grad_lo=g_lo,
        pick=np.concatenate([pick, pick], 0).astype(jnp.bfloat16),
        first=np.concatenate([high, high], 0),
        first_lo=low,
        second_a=second[0],
        second_b=second[1],
        ta_hi=t_hi,
        ta_lo=t_lo,
        tb_hi=np.concatenate([t_hi[:, :XL], moved[0]], 1),
        tb_lo=np.concatenate([t_lo[:, :XL], moved[1]], 1),
        t_both=np.concatenate([t_hi[:, :XL], t_lo[:, :XL]], 1),
    )


def smoothing_tables():
    offsets = np.arange(3 * XL)[:, None] - XL - np.arange(XL)[None, :]
    sigma_x = XL / 2.0
    gauss_x = np.exp(-0.5 * (offsets / sigma_x) ** 2) * (np.abs(offsets) <= XL)
    normal_x = np.exp(-0.5 * (np.arange(-XL, XL + 1) / sigma_x) ** 2).sum()
    distance = np.arange(YP)[:, None] - np.arange(YP)[None, :]
    gauss_y = np.exp(-0.5 * (distance / SIGMA_Y) ** 2)
    gauss_y = gauss_y / gauss_y.sum(axis=1, keepdims=True)
    return gauss_x / normal_x, gauss_y


def apply5(m, x):
    e0, o0, e1, o1, mid = x[0] + x[4], x[0] - x[4], x[1] + x[3], x[1] - x[3], x[2]
    f = lambda v: np.float32(v)
    odd = [
        f((m[a, 0] + m[a, 4]) / 2) * e0 + f((m[a, 1] + m[a, 3]) / 2) * e1 + f(m[a, 2]) * mid
        for a in (0, 1)
    ]
    even = [
        f((m[a, 0] - m[a, 4]) / 2) * o0 + f((m[a, 1] - m[a, 3]) / 2) * o1 for a in (0, 1, 2)
    ]
    return [even[0] + odd[0], even[1] + odd[1], even[2], even[1] - odd[1], even[0] - odd[0]]


def apply_y(fields, kappa):
    row = lax.broadcasted_iota(jnp.int32, (8, XL), 0)

    def plane(z, carry):
        at = lambda a: pl.ds(a, 8, stride=4)
        k = [kappa[z, at(a), :] for a in range(5)]
        for v, out in fields:
            g = apply5(APPLY, [v[z, at(a), :] for a in range(5)])
            o = apply5(GATHER, [k[a] * g[a] for a in range(5)])
            moved = pltpu.roll(o[4], 1, 0)
            out[z, at(0), :] = jnp.where(row == 0, 2.0 * o[0], o[0] + moved)
            for b in range(1, 4):
                out[z, at(b), :] = o[b]
            out[z, 32:33, :] = 2.0 * moved[0:1]
        return carry

    lax.fori_loop(0, ZP, plane, 0, unroll=UNROLL_Y)


def apply_z(fields, kappa, use):
    def block(rows):
        for i, v in enumerate(fields):
            ends = None
            for e in range(4):
                g = apply5(APPLY, [v[4 * e + a, rows, :] for a in range(5)])
                o = apply5(GATHER, [kappa[4 * e + a, rows, :] * g[a] for a in range(5)])
                use(i, 4 * e, rows, 2.0 * o[0] if e == 0 else o[0] + ends)
                for b in range(1, 4):
                    use(i, 4 * e + b, rows, o[b])
                ends = o[4]
            use(i, 16, rows, 2.0 * ends)

    def step(j, carry):
        block(pl.ds(pl.multiple_of(8 * j, 8), 8))
        return carry

    lax.fori_loop(0, 4, step, 0, unroll=UNROLL_Z)
    block(pl.ds(32, 1))


def inverse_weight(i, last):
    node = i & 3
    end = (i == 0) | (i == last)
    inner = jnp.where(node == 2, np.float32(1.0 / SHARED[2]), np.float32(1.0 / SHARED[1]))
    shared = jnp.where(end, np.float32(2.0 / SHARED[0]), np.float32(1.0 / SHARED[0]))
    return jnp.where(node == 0, shared, inner)


def add_forcing(target, c_ref, index, source, instant):
    lane = lax.broadcasted_iota(jnp.int32, (1, XL), 1)
    node = lane % 4
    inv_x = jnp.where(
        node == 0, 1.0 / SHARED[0], jnp.where(node == 2, 1.0 / SHARED[2], 1.0 / SHARED[1])
    ).astype(jnp.float32)
    for r in range(16):
        point = index[r]
        row = lax.shift_right_logical(point, 7)
        z = lax.shift_right_logical(row * 1986, 16)
        y = row - z * YP
        amount = source[instant, r] * inverse_weight(z, ZP - 1) * inverse_weight(y, YP - 1)
        at = (pl.ds(z, 1), pl.ds(y, 1), slice(None))
        change = jnp.where(lane == (point & (XL - 1)), inv_x * amount, 0.0)
        target[at] = target[at] + c_ref[at] * change[None]


def flip_rows(source, target, flag):
    for y in range(YP):
        to = jnp.where(flag != 0, 32 - y, y)
        target[:, pl.ds(to, 1), :] = source[:, y : y + 1, :]


def pack_edges(a, b, ka, ap, bp, c, f, edges):
    rows = slice(0, YP)
    lane = lax.broadcasted_iota(jnp.int32, (YP, XL), 1)
    first = (0, LANE_B, LANE_K, LANE_PA, LANE_CA, LANE_PB, LANE_CB)
    for i in range(PLANES):
        whole = [None] * len(edges)
        for g in range(3):
            z = PLANES * g + i
            if z >= ZP:
                continue
            av, bv, k, cv = a[z, rows, :], b[z, rows, :], ka[z, rows, :], c[z, rows, :]
            pa = 2.0 * av - ap[z, rows, :] + f[z, rows, :]
            pb = 2.0 * bv - bp[z, rows, :]
            for n, (to_after, _) in enumerate(edges):
                tile = None
                for j, value in reversed(list(enumerate((av, bv, k, pa, cv, pb, cv)))):
                    moved = pltpu.roll(value, first[j] + 8 * to_after + GROUP * g, 1)
                    if tile is None:
                        tile = moved
                    else:
                        above = first[j + 1] + (4 * to_after if j + 1 > 2 else 0)
                        tile = jnp.where(lane < GROUP * g + above, moved, tile)
                whole[n] = tile if g == 0 else jnp.where(lane < GROUP * g, whole[n], tile)
        for n, (_, pack) in enumerate(edges):
            pack[i, :, :] = whole[n]


def pack_kernel(
    flip, odd, an_in, bn_in, ap_in, bp_in, ka_in, de_in, index_in, source_in,
    far_out, near_out, an, bn, ap, bp, ka, c_out, f_out, de, far_pack, near_pack, index, source, sem,
):
    rows = slice(0, YP)
    scalars = []
    for i, (src, dst) in enumerate(((index_in, index), (source_in, source))):
        scalars.append(pltpu.make_async_copy(src, dst, sem.at[6 + i]))
        scalars[-1].start()
    copies = [
        pltpu.make_async_copy(de_in, de.at[:, rows, :], sem.at[0]),
        pltpu.make_async_copy(ka_in, ka.at[:, rows, :], sem.at[1]),
    ]
    for i, (src, dst) in enumerate(((an_in, an), (bn_in, bn), (ap_in, ap), (bp_in, bp))):
        copies.append(pltpu.make_async_copy(src.at[:, :, 0, :], dst.at[:, rows, :], sem.at[2 + i]))
    for copy in copies:
        copy.start()
    f_out[...] = jnp.zeros_like(f_out)
    for copy in scalars:
        copy.wait()
    copies[0].wait()
    for z in range(ZP):
        c_out[z, 0:YP, :] = DT2 / de[z, 0:YP, :]
    add_forcing(f_out, c_out, index, source, 0)
    for copy in copies[1:]:
        copy.wait()
    edges = [(odd[0], far_pack), (1 - odd[0], near_pack)]
    pack_edges(an, bn, ka, ap, bp, c_out, f_out, edges)
    flip_rows(far_pack, far_out, flip[0] * odd[0])
    flip_rows(near_pack, near_out, flip[0] * (1 - odd[0]))


def dot(a, b):
    return jnp.dot(a, b, preferred_element_type=jnp.float32)


def halves(x):
    hi = x.astype(jnp.bfloat16)
    return hi, (x - hi.astype(jnp.float32)).astype(jnp.bfloat16)


def dot3(x, m_hi, m_lo):
    hi, lo = halves(x)
    return dot(hi, m_hi) + dot(lo, m_hi) + dot(hi, m_lo)


def flat(ref):
    return ref[...].reshape(ROWS, ref.shape[-1])


def local_kernel(
    a, b, ka, c, f, grad, grad_lo, pick, index_in, source_in,
    a_out, b_out, f1_out, ga_out, gb_out, kg_out, index, source, sem,
):
    scalars = []
    for i, (src, dst) in enumerate(((index_in, index), (source_in, source))):
        scalars.append(pltpu.make_async_copy(src, dst, sem.at[i]))
        scalars[-1].start()
    apply_y(((a, a_out), (b, b_out)), ka)

    def use(i, z, rows, value):
        out = (a_out, b_out)[i]
        total = c[z, rows, :] * (out[z, rows, :] + value)
        out[z, rows, :] = f[z, rows, :] - total if i == 0 else -total

    apply_z((a, b), ka, use)
    f1_out[...] = jnp.zeros_like(f1_out)
    for copy in scalars:
        copy.wait()
    add_forcing(f1_out, c, index, source, 1)
    for field, out in ((a, ga_out), (b, gb_out)):
        hi, lo = halves(flat(field))
        out[...] = dot(jnp.concatenate([hi, lo], 1), grad[...]) + dot(hi, grad_lo[...])
    hi, lo = halves(flat(ka))
    kg_out[...] = dot(jnp.concatenate([hi, lo], 1), pick[...])


def step_kernel(
    flip, odd, an, ap, bn, bp, ka, c, a0, b0, f1, ga, gb, kg0, far_in, near_in,
    first, first_lo, grad, second_a, ta_hi, ta_lo, tb_hi, tb_lo, t_both,
    k_out, al_out, bl_out, v2a, v1b, u1_out, kg,
    left, raw, u, ku, cu, qu, wa, wb, y1, v1a, k, sem,
):
    lane = lax.broadcasted_iota(jnp.int32, (YP, XL), 1)
    rows = slice(0, YP)
    sent = []

    def send(src, dst, dense):
        if dense:
            src, dst = src.at[:, rows, :], dst.at[:, :, 0, :]
        sent.append(pltpu.make_async_copy(src, dst, sem.at[len(sent)]))
        sent[-1].start()

    is_odd = odd[0] != 0
    raw[...] = jnp.where(is_odd, far_in[...], near_in[...])
    flip_rows(raw, left, flip[0])
    own_a = (lane & 63) < LANE_B
    for z in range(ZP):
        i, at = z % PLANES, GROUP * (z // PLANES)
        before = jnp.where(is_odd, near_in[i], far_in[i])
        if at:
            before = pltpu.roll(before, XL - at, 1)
        tile = jnp.where(lane < AFTER, before, pltpu.roll(left[i], (AFTER - at) % XL, 1))
        u[z, rows, :] = tile
        ku[z, rows, :] = jnp.where(
            own_a, pltpu.roll(tile, XL - LANE_K, 1), pltpu.roll(tile, XL - LANE_K + LANE_B, 1)
        )
        qu[z, rows, :] = pltpu.roll(tile, XL - LANE_PA, 1)
        cu[z, rows, :] = pltpu.roll(tile, XL - LANE_CA, 1)
    apply_y(((u, y1),), ku)

    def use(i, z, rows, value):
        qu[z, rows, :] = qu[z, rows, :] - cu[z, rows, :] * (y1[z, rows, :] + value)

    apply_z((u,), ku, use)

    lane2 = lax.broadcasted_iota(jnp.int32, (ROWS, XL), 1)
    tall = lambda value: value.reshape(ZP, YPAD, value.shape[-1])
    hi, lo = halves(flat(u))
    edge = dot(jnp.concatenate([hi, lo], 1), first[...]) + dot(hi, first_lo[...])
    kg[...] = jnp.concatenate([flat(ka), kg0[...] + edge[:, 4 * XL :]], 1)
    xa = dot3((ga[...] + edge[:, 0 : 2 * XL]) * kg[...], ta_hi[...], ta_lo[...])
    xb = dot3((gb[...] + edge[:, 2 * XL : 4 * XL]) * kg[...], tb_hi[...], tb_lo[...])
    u1 = flat(qu) - flat(cu) * (xa[:, XL:] + xb[:, XL:])
    hi = u1.astype(jnp.bfloat16).astype(jnp.float32)
    packed = jnp.where(
        (lane2 & 63) < 16,
        hi,
        jnp.where((lane2 & 63) < 32, pltpu.roll(u1 - hi, 16, 1), pltpu.roll(hi, 32, 1)),
    ).astype(jnp.bfloat16)
    u1_out[...] = packed
    wa[...] = tall(xa[:, 0:XL])
    wb[...] = tall(xb[:, 0:XL])
    for z in range(ZP):
        cz = c[z, rows, :]
        acc_a = a0[z, rows, :] - cz * wa[z, rows, :]
        acc_b = b0[z, rows, :] - cz * wb[z, rows, :]
        a, b = an[z, rows, :], bn[z, rows, :]
        v1a[z, rows, :] = 2.0 * a - ap[z, rows, :] + acc_a
        v1b[z, rows, :] = 2.0 * b - bp[z, rows, :] + acc_b
        ku[z, rows, :] = b * acc_a
    send(v1a, al_out, True)
    send(v1b, bl_out, True)
    apply_y(((v1a, y1),), ka)

    def add(i, z, rows, value):
        y1[z, rows, :] = y1[z, rows, :] + value

    apply_z((v1a,), ka, add)
    wa[...] = tall(second_x(v1a, packed, grad, second_a, kg, t_both))
    for i in (6, 7):
        k[72 * i + 64 : 72 * i + 72, :] = jnp.zeros((8, XL), jnp.float32)
    for z in (ZP - 1, *range(ZP - 1)):
        acc_a = f1[z, rows, :] - c[z, rows, :] * (wa[z, rows, :] + y1[z, rows, :])
        v2a[z, rows, :] = 2.0 * v1a[z, rows, :] - an[z, rows, :] + acc_a
        t = ku[z, rows, :] + v1b[z, rows, :] * acc_a
        if z < ZP - 1:
            at = 72 * (z // 2) + 32 * (z % 2)
            k[at : at + 8, :] = t[0:8]
            k[at + 8 : at + 16, :] = t[25:33]
            k[at + 16 : at + 24, :] = t[8:16]
            k[at + 24 : at + 32, :] = t[17:25]
        else:
            for i in range(4):
                at = 72 * i + 64
                k[at : at + 4, :] = t[4 * i : 4 * i + 4]
                k[at + 4 : at + 8, :] = t[29 - 4 * i : 33 - 4 * i]
        at = 72 * (4 + z // 8) + 64 + z % 8
        k[at : at + 1, :] = t[16:17]
        for j in {1: [0], 3: [1], 5: [2], 7: [3], 9: [4], 13: [6], 15: [5, 7]}.get(z, []):
            at = pl.ds(72 * j, 72)
            send(k.at[at], k_out.at[at], False)
    for copy in sent:
        copy.wait()


def second_x(v, packed, grad, second, kg, t_both):
    hi, lo = halves(flat(v))
    g = dot(jnp.concatenate([hi, lo], 1), grad[...])
    g = g + dot(jnp.concatenate([hi, packed], 1), second[...])
    hi, lo = halves(g * kg[...])
    both = dot(hi, t_both[...])
    return both[:, 0:XL] + both[:, XL:] + dot(lo, t_both[:, 0:XL])


def last_kernel(bn, ka, c, v1b, v2a, u1, kg, grad, second_b, t_both, af_out, bf_out, y1, wb, sem):
    rows = slice(0, YP)
    first = pltpu.make_async_copy(v2a.at[:, rows, :], af_out.at[:, :, 0, :], sem.at[1])
    first.start()
    apply_y(((v1b, y1),), ka)

    def add(i, z, rows, value):
        y1[z, rows, :] = y1[z, rows, :] + value

    apply_z((v1b,), ka, add)
    x = second_x(v1b, u1[...], grad, second_b, kg, t_both)
    wb[...] = x.reshape(ZP, YPAD, XL)
    for z in range(ZP):
        acc = c[z, rows, :] * (wb[z, rows, :] + y1[z, rows, :])
        wb[z, rows, :] = 2.0 * v1b[z, rows, :] - bn[z, rows, :] - acc
    copy = pltpu.make_async_copy(wb.at[:, rows, :], bf_out.at[:, :, 0, :], sem.at[0])
    copy.start()
    first.wait()
    copy.wait()


def turn(part, whole, flipped):
    for i in range(part // 72):
        for r in range(8):
            for j in range(9):
                at = 72 * i + 8 * (j ^ 1 if j < 8 else j) + 7 - r
                flipped[72 * i + 8 * j + r : 72 * i + 8 * j + r + 1, :] = whole[at : at + 1, :]


def turned_part(group, value, flipped):
    row = lax.broadcasted_iota(jnp.int32, value.shape, 0)
    stays = (row % 72 >= 64) & (row // 72 + group[0] * (value.shape[0] // 72) >= 4)
    return jnp.where(stays, value, flipped[...])


def sum_kernel(flip, group, odd, parts, far_out, near_out, own_out, flipped):
    total = parts[0]
    for i in range(1, parts.shape[0]):
        total = total + parts[i]
    own_out[...] = total
    turn(total.shape[0], own_out, flipped)
    other = turned_part(group, total, flipped)
    turned = flip[0] != 0
    far_out[...] = jnp.where(turned & (odd[0] != 0), other, total)
    near_out[...] = jnp.where(turned & (odd[0] == 0), other, total)


def smooth_kernel(flip, group, odd, far_in, own, near_in, gx_hi, gx_lo, out, done, flipped, sem):
    is_odd = odd[0] != 0
    before = jnp.where(is_odd, near_in[...], far_in[...])
    after = jnp.where(is_odd, far_in[...], near_in[...])
    done[...] = after
    turn(after.shape[0], done, flipped)
    after = jnp.where(flip[0] != 0, turned_part(group, after, flipped), after)
    total = None
    for i, part in enumerate((before, own[...], after)):
        at = slice(XL * i, XL * (i + 1))
        one = dot3(part, gx_hi[at, :], gx_lo[at, :])
        total = one if total is None else total + one
    done[...] = total
    copies = [pltpu.make_async_copy(done, out.at[i], sem.at[i]) for i in range(out.shape[0])]
    for copy in copies:
        copy.start()
    for copy in copies:
        copy.wait()


def finish_kernel(t, blocks_hi, blocks_lo, end_hi, end_lo, middle, out, rows, done_all, sem):
    def planes(first, n, m_hi, m_lo):
        if n > 1:
            for i in range(n):
                at = 72 * ((first + i) // 2) + 32 * (i % 2)
                rows[32 * i : 32 * i + 32, :] = t[at : at + 32, :]
        else:
            for i in range(4):
                rows[8 * i : 8 * i + 8, :] = t[72 * i + 64 : 72 * i + 72, :]
        hi, lo = halves(rows[0 : 32 * n, :])
        done = dot(m_hi[...], hi) + dot(m_hi[...], lo) + dot(m_lo[...], hi)
        for i in range(n):
            z = first + i
            at = 72 * (4 + z // 8) + 64 + z % 8
            done_all[z] = done[i * YPAD : (i + 1) * YPAD] + middle[...] * t[at : at + 1, :]
        at = pl.ds(first, n)
        copy = pltpu.make_async_copy(done_all.at[at, 0:YP, :], out.at[at], sem.at[first // 8])
        copy.start()
        return copy

    copies = [planes(0, 8, blocks_hi, blocks_lo), planes(8, 8, blocks_hi, blocks_lo), planes(16, 1, end_hi, end_lo)]
    for copy in copies:
        copy.wait()


SMEM_SPEC = pl.BlockSpec(memory_space=pltpu.SMEM)
VMEM_SPEC = pl.BlockSpec(memory_space=pltpu.VMEM)
ANY_SPEC = pl.BlockSpec(memory_space=pl.ANY)


def near(*shape, dtype=jnp.float32):
    return pltpu.VMEM(shape, dtype)


def distant(*shape, dtype=jnp.float32):
    return pltpu.HBM(shape, dtype)


def call(kernel, outs, scalars, arrays, scratch=(), far=(), flops=0, moved=0, limit=24):
    far = [pltpu.with_memory_space_constraint(v, pltpu.HBM) for v in far]
    out_specs = [ANY_SPEC if o.memory_space == pltpu.HBM else VMEM_SPEC for o in outs]
    return pl.pallas_call(
        kernel,
        out_shape=outs,
        in_specs=[SMEM_SPEC] * len(scalars) + [VMEM_SPEC] * len(arrays) + [ANY_SPEC] * len(far),
        out_specs=out_specs,
        scratch_shapes=list(scratch),
        compiler_params=pltpu.CompilerParams(vmem_limit_bytes=limit * 1024 * 1024),
        cost_estimate=pl.CostEstimate(flops=flops, bytes_accessed=moved, transcendentals=0),
    )(*scalars, *arrays, *far)


def swap(value, odd):
    n = lax.axis_size("cuts")
    return lax.ppermute(value, "cuts", [(i, (i + 1 if i % 2 == odd else i - 1) % n) for i in range(n)])


def local(an, ap, bn, bp, kappa, density, flip, index, source):
    dense, padded, edge = distant(ZP, YP, 1, XL), near(ZP, YPAD, XL), near(PLANES, YP, XL)
    odd = (lax.axis_index("cuts").astype(jnp.int32) % 2).reshape(1)
    src = source[0]
    tab = {name: jnp.asarray(value) for name, value in tables().items()}
    fields = [v.reshape(ZP, YP, 1, XL) for v in (an, bn, ap, bp)]
    dma = pltpu.SemaphoreType.DMA
    receivers = [pltpu.SMEM(v.shape, v.dtype) for v in (index, src)]
    to_far, to_near, an, bn, ap, bp, ka, c, f0 = call(
        pack_kernel,
        [edge, edge] + [padded] * 7,
        [flip, odd],
        [],
        [padded, edge, edge, *receivers, dma((8,))],
        far=[*fields, kappa, density, index, src],
        moved=4_000_000,
    )
    from_far = swap(to_far, 1)
    wide, narrow = near(ROWS, 2 * XL), near(ROWS, XL)
    from_near = swap(to_near, 0)
    a0, b0, f1, ga, gb, kg0 = call(
        local_kernel,
        [padded, padded, padded, wide, wide, narrow],
        [],
        [an, bn, ka, c, f0, tab["grad"], tab["grad_lo"], tab["pick"]],
        [*receivers, dma((2,))],
        far=[index, src],
        flops=300_000_000,
        moved=5_000_000,
    )
    packed = near(ROWS, XL, dtype=jnp.bfloat16)
    k, al, bl, v2a, v1b, u1, kg = call(
        step_kernel,
        [distant(KROWS, XL), dense, dense, padded, padded, packed, wide],
        [flip, odd],
        [an, ap, bn, bp, ka, c, a0, b0, f1, ga, gb, kg0, from_far, from_near]
        + [tab[n] for n in ("first", "first_lo", "grad", "second_a", "ta_hi", "ta_lo", "tb_hi", "tb_lo", "t_both")],
        [edge, edge] + [padded] * 8 + [near(KROWS, XL), dma((10,))],
        flops=600_000_000,
        moved=6_000_000,
    )
    groups = lax.axis_size("event")
    part = KROWS // groups
    parts = lax.all_to_all(k.reshape(groups, part, XL), "event", 0, 0)
    af, bf = call(
        last_kernel,
        [dense, dense],
        [],
        [bn, ka, c, v1b, v2a, u1, kg, tab["grad"], tab["second_b"], tab["t_both"]],
        [padded, padded, dma((2,))],
        flops=300_000_000,
        moved=5_000_000,
    )
    outs = (af, al, bf, bl)
    group = lax.axis_index("event").astype(jnp.int32).reshape(1)
    place = [flip, group, odd]
    to_far, to_near, total = call(sum_kernel, [near(part, XL)] * 3, place, [parts], [near(part, XL)])
    from_near = swap(to_near, 0)
    from_far = swap(to_far, 1)
    gauss_x, gauss_y = smoothing_tables()
    gauss = [jnp.asarray(v) for v in split(gauss_x)]
    spread = call(
        smooth_kernel,
        [distant(groups, part, XL)],
        place,
        [from_far, total, from_near, *gauss],
        [near(part, XL), near(part, XL), dma((8,))],
    )[0]
    whole = lax.all_to_all(spread, "event", 0, 0).reshape(KROWS, XL)
    order = [*range(0, 8), *range(25, 33), *range(8, 16), *range(17, 25)]
    blocks, end, middle = np.zeros((8 * YPAD, 256)), np.zeros((YPAD, 32)), np.zeros((YPAD, XL))
    for i in range(8):
        blocks[i * YPAD : i * YPAD + YP, i * 32 : i * 32 + 32] = gauss_y[:, order]
    end[0:YP] = gauss_y[:, [y for i in range(0, 16, 4) for y in (*range(i, i + 4), *range(29 - i, 33 - i))]]
    middle[0:YP] = gauss_y[:, 16:17]
    smoothed = call(
        finish_kernel,
        [distant(ZP, YP, XL)],
        [],
        [whole, *(jnp.asarray(v) for v in (*split(blocks), *split(end))), jnp.asarray(middle, jnp.float32)],
        [near(256, XL), near(ZP, YPAD, XL), dma((3,))],
    )[0]
    return *(v.reshape(1, ZP, YP, XL) for v in outs), smoothed


def solution(mesh):
    field = P("event", None, None, "cuts")
    grid = P(None, None, "cuts")
    return jax.shard_map(
        local,
        mesh=mesh,
        in_specs=(field,) * 4 + (grid, grid, P("cuts"), P("cuts"), P("event", None, "cuts")),
        out_specs=(field,) * 4 + (grid,),
        check_vma=False,
    )
```

```python
import jax
import jax.numpy as jnp
import numpy as np
from jax import lax
from jax.experimental import pallas as pl
from jax.experimental.pallas import tpu as pltpu
from jax.sharding import PartitionSpec as P

DT2 = 0.003
SIGMA_Y = 1.0
ZP, YP, XL = 17, 33, 128
YPAD = 40
ROWS = ZP * YPAD
PLANES, GROUP = 6, 42
KROWS = 576
UNROLL_Y, UNROLL_Z = 17, 4


def gll_tables():
    nodes = np.array([-1.0, -np.sqrt(3.0 / 7.0), 0.0, np.sqrt(3.0 / 7.0), 1.0])
    weights = np.array([0.1, 49.0 / 90.0, 32.0 / 45.0, 49.0 / 90.0, 0.1])
    deriv = np.zeros((5, 5))
    for a in range(5):
        for b in range(5):
            for m in range(5):
                if m == b:
                    continue
                factor = 1.0 / (nodes[b] - nodes[m])
                for k in range(5):
                    if k == b or k == m:
                        continue
                    factor = factor * (nodes[a] - nodes[k]) / (nodes[b] - nodes[k])
                deriv[a, b] += factor
    return weights, deriv


GW, GD = gll_tables()
SHARED = np.array([0.2, GW[1], GW[2], GW[3], 0.2])
APPLY = GW[:, None] * GD
GATHER = (GD / SHARED[None, :]).T


def split(m):
    hi = np.asarray(m, np.float32).astype(jnp.bfloat16)
    lo = (np.asarray(m, np.float32) - hi.astype(np.float32)).astype(jnp.bfloat16)
    return hi, lo


LANE_B, LANE_K, LANE_PA, LANE_CA, LANE_PB, LANE_CB = 8, 16, 21, 25, 29, 33
AFTER = 64


def x_tables():
    def node(e, a):
        if 0 <= e < 32:
            return 4 * e + a if a < 4 else XL + e
        return XL + {-1: 32, -2: 37, 32: 42}[e] + a

    def halo(c):
        return c + 8 if c < 0 else AFTER + c - XL

    grad, edge = np.zeros((XL, 2 * XL)), np.zeros((XL, 2 * XL))
    back = np.zeros((2 * XL, 2 * XL))
    pick, pick_edge = np.zeros((XL, XL)), np.zeros((XL, XL))
    for e in range(-2, 33):
        for a in range(5):
            n = node(e, a)
            for b in range(5):
                c = 4 * e + b
                own = 0 <= c < XL
                (grad if own else edge)[c if own else halo(c), n] += APPLY[a, b]
                if -4 <= c <= XL:
                    back[n, c if own else XL + halo(c)] += GATHER[b, a]
            if n >= XL:
                c = 4 * e + a
                if 0 <= c < XL:
                    pick[c, n - XL] = 1.0
                else:
                    pick_edge[LANE_K + halo(c), n - XL] = 1.0
    return grad, edge, back, pick, pick_edge


def tables():
    grad, edge, back, pick, pick_edge = x_tables()
    g_hi, g_lo = split(grad)
    e_hi, e_lo = split(edge)
    high, low = np.zeros((XL, 5 * XL), jnp.bfloat16), np.zeros((XL, 5 * XL), jnp.bfloat16)
    for m, part in ((high, e_hi), (low, e_lo)):
        m[:, 0 : 2 * XL] = part
        m[:, 2 * XL : 4 * XL] = np.roll(part, LANE_B, 0)
    high[:, 4 * XL :] = pick_edge.astype(jnp.bfloat16)
    second = []
    for at in (0, LANE_B):
        m = np.zeros((XL, 2 * XL), jnp.bfloat16)
        for i, part in enumerate((e_hi, e_hi, e_lo)):
            for lane in (4, 5, 6, 7, AFTER):
                m[16 * i + at + lane] = part[lane]
        second.append(np.concatenate([g_lo, m], 0))
    t_hi, t_lo = split(back)
    moved = [np.roll(t[:, XL:], LANE_B, 1) for t in (t_hi, t_lo)]
    return dict(
        grad=np.concatenate([g_hi] * 2, 0),
        grad_lo=g_lo,
        pick=np.concatenate([pick, pick], 0).astype(jnp.bfloat16),
        first=np.concatenate([high, high], 0),
        first_lo=low,
        second_a=second[0],
        second_b=second[1],
        ta_hi=t_hi,
        ta_lo=t_lo,
        tb_hi=np.concatenate([t_hi[:, :XL], moved[0]], 1),
        tb_lo=np.concatenate([t_lo[:, :XL], moved[1]], 1),
        t_both=np.concatenate([t_hi[:, :XL], t_lo[:, :XL]], 1),
    )


def smoothing_tables():
    offsets = np.arange(3 * XL)[:, None] - XL - np.arange(XL)[None, :]
    sigma_x = XL / 2.0
    gauss_x = np.exp(-0.5 * (offsets / sigma_x) ** 2) * (np.abs(offsets) <= XL)
    normal_x = np.exp(-0.5 * (np.arange(-XL, XL + 1) / sigma_x) ** 2).sum()
    distance = np.arange(YP)[:, None] - np.arange(YP)[None, :]
    gauss_y = np.exp(-0.5 * (distance / SIGMA_Y) ** 2)
    gauss_y = gauss_y / gauss_y.sum(axis=1, keepdims=True)
    return gauss_x / normal_x, gauss_y


def apply5(m, x):
    e0, o0, e1, o1, mid = x[0] + x[4], x[0] - x[4], x[1] + x[3], x[1] - x[3], x[2]
    f = lambda v: np.float32(v)
    odd = [
        f((m[a, 0] + m[a, 4]) / 2) * e0 + f((m[a, 1] + m[a, 3]) / 2) * e1 + f(m[a, 2]) * mid
        for a in (0, 1)
    ]
    even = [
        f((m[a, 0] - m[a, 4]) / 2) * o0 + f((m[a, 1] - m[a, 3]) / 2) * o1 for a in (0, 1, 2)
    ]
    return [even[0] + odd[0], even[1] + odd[1], even[2], even[1] - odd[1], even[0] - odd[0]]


def apply_y(fields, kappa):
    row = lax.broadcasted_iota(jnp.int32, (8, XL), 0)

    def plane(z, carry):
        at = lambda a: pl.ds(a, 8, stride=4)
        k = [kappa[z, at(a), :] for a in range(5)]
        for v, out in fields:
            g = apply5(APPLY, [v[z, at(a), :] for a in range(5)])
            o = apply5(GATHER, [k[a] * g[a] for a in range(5)])
            moved = pltpu.roll(o[4], 1, 0)
            out[z, at(0), :] = jnp.where(row == 0, 2.0 * o[0], o[0] + moved)
            for b in range(1, 4):
                out[z, at(b), :] = o[b]
            out[z, 32:33, :] = 2.0 * moved[0:1]
        return carry

    lax.fori_loop(0, ZP, plane, 0, unroll=UNROLL_Y)


def apply_z(fields, kappa, use):
    def block(rows):
        for i, v in enumerate(fields):
            ends = None
            for e in range(4):
                g = apply5(APPLY, [v[4 * e + a, rows, :] for a in range(5)])
                o = apply5(GATHER, [kappa[4 * e + a, rows, :] * g[a] for a in range(5)])
                use(i, 4 * e, rows, 2.0 * o[0] if e == 0 else o[0] + ends)
                for b in range(1, 4):
                    use(i, 4 * e + b, rows, o[b])
                ends = o[4]
            use(i, 16, rows, 2.0 * ends)

    def step(j, carry):
        block(pl.ds(pl.multiple_of(8 * j, 8), 8))
        return carry

    lax.fori_loop(0, 4, step, 0, unroll=UNROLL_Z)
    block(pl.ds(32, 1))


def inverse_weight(i, last):
    node = i & 3
    end = (i == 0) | (i == last)
    inner = jnp.where(node == 2, np.float32(1.0 / SHARED[2]), np.float32(1.0 / SHARED[1]))
    shared = jnp.where(end, np.float32(2.0 / SHARED[0]), np.float32(1.0 / SHARED[0]))
    return jnp.where(node == 0, shared, inner)


def add_forcing(target, c_ref, index, source, instant):
    lane = lax.broadcasted_iota(jnp.int32, (1, XL), 1)
    node = lane % 4
    inv_x = jnp.where(
        node == 0, 1.0 / SHARED[0], jnp.where(node == 2, 1.0 / SHARED[2], 1.0 / SHARED[1])
    ).astype(jnp.float32)
    for r in range(16):
        point = index[r]
        row = lax.shift_right_logical(point, 7)
        z = lax.shift_right_logical(row * 1986, 16)
        y = row - z * YP
        amount = source[instant, r] * inverse_weight(z, ZP - 1) * inverse_weight(y, YP - 1)
        at = (pl.ds(z, 1), pl.ds(y, 1), slice(None))
        change = jnp.where(lane == (point & (XL - 1)), inv_x * amount, 0.0)
        target[at] = target[at] + c_ref[at] * change[None]


def flip_rows(source, target, flag):
    for y in range(YP):
        to = jnp.where(flag != 0, 32 - y, y)
        target[:, pl.ds(to, 1), :] = source[:, y : y + 1, :]


def pack_edges(a, b, ka, ap, bp, c, f, is_odd, far_pack, near_pack):
    rows = slice(0, YP)
    lane = lax.broadcasted_iota(jnp.int32, (YP, XL), 1)
    first = (0, LANE_B, LANE_K, LANE_PA, LANE_CA, LANE_PB, LANE_CB)
    for i in range(PLANES):
        before = after = None
        for g in range(3):
            z, base = PLANES * g + i, GROUP * g
            if z >= ZP:
                continue
            av, bv, k, cv = a[z, rows, :], b[z, rows, :], ka[z, rows, :], c[z, rows, :]
            pa = 2.0 * av - ap[z, rows, :] + f[z, rows, :]
            pb = 2.0 * bv - bp[z, rows, :]
            moved = [
                pltpu.roll(v, at + base, 1) if at + base else v
                for v, at in zip((av, bv, k, pa, cv, pb, cv), first)
            ]
            to_before = to_after = moved[6]
            for j in reversed(range(6)):
                to_before = jnp.where(lane < base + first[j + 1], moved[j], to_before)
                above = base + first[j + 1] - (4 if j >= 2 else 8)
                covered = lane < above if above else lane >= XL - 8
                to_after = jnp.where(covered, moved[j], to_after)
            if g == 0:
                before, after = to_before, to_after
            else:
                before = jnp.where(lane < base, before, to_before)
                after = jnp.where((lane < base - 8) | (lane >= XL - 8), after, to_after)
        after = pltpu.roll(after, 8, 1)
        far_pack[i, :, :] = jnp.where(is_odd, after, before)
        near_pack[i, :, :] = jnp.where(is_odd, before, after)


def pack_kernel(
    flip, odd, an_in, bn_in, ap_in, bp_in, ka_in, de_in, index_in, source_in,
    far_out, near_out, an, bn, ap, bp, ka, c_out, f_out, de, far_pack, near_pack, index, source, sem,
):
    rows = slice(0, YP)
    scalars = []
    for i, (src, dst) in enumerate(((index_in, index), (source_in, source))):
        scalars.append(pltpu.make_async_copy(src, dst, sem.at[6 + i]))
        scalars[-1].start()
    copies = [
        pltpu.make_async_copy(de_in, de.at[:, rows, :], sem.at[0]),
        pltpu.make_async_copy(ka_in, ka.at[:, rows, :], sem.at[1]),
    ]
    for i, (src, dst) in enumerate(((an_in, an), (bn_in, bn), (ap_in, ap), (bp_in, bp))):
        copies.append(pltpu.make_async_copy(src.at[:, :, 0, :], dst.at[:, rows, :], sem.at[2 + i]))
    for copy in copies:
        copy.start()
    f_out[...] = jnp.zeros_like(f_out)
    for copy in scalars:
        copy.wait()
    copies[0].wait()
    for z in range(ZP):
        c_out[z, 0:YP, :] = DT2 / de[z, 0:YP, :]
    add_forcing(f_out, c_out, index, source, 0)
    for copy in copies[1:]:
        copy.wait()
    pack_edges(an, bn, ka, ap, bp, c_out, f_out, odd[0] != 0, far_pack, near_pack)
    flip_rows(far_pack, far_out, flip[0] * odd[0])
    flip_rows(near_pack, near_out, flip[0] * (1 - odd[0]))


def dot(a, b):
    return jnp.dot(a, b, preferred_element_type=jnp.float32)


def halves(x):
    hi = x.astype(jnp.bfloat16)
    return hi, (x - hi.astype(jnp.float32)).astype(jnp.bfloat16)


def dot3(x, m_hi, m_lo):
    hi, lo = halves(x)
    return dot(hi, m_hi) + dot(lo, m_hi) + dot(hi, m_lo)


def flat(ref):
    return ref[...].reshape(ROWS, ref.shape[-1])


def local_kernel(
    a, b, ka, c, f, grad, grad_lo, pick, index_in, source_in,
    a_out, b_out, f1_out, ga_out, gb_out, kg_out, index, source, sem,
):
    scalars = []
    for i, (src, dst) in enumerate(((index_in, index), (source_in, source))):
        scalars.append(pltpu.make_async_copy(src, dst, sem.at[i]))
        scalars[-1].start()
    apply_y(((a, a_out), (b, b_out)), ka)

    def use(i, z, rows, value):
        out = (a_out, b_out)[i]
        total = c[z, rows, :] * (out[z, rows, :] + value)
        out[z, rows, :] = f[z, rows, :] - total if i == 0 else -total

    apply_z((a, b), ka, use)
    f1_out[...] = jnp.zeros_like(f1_out)
    for copy in scalars:
        copy.wait()
    add_forcing(f1_out, c, index, source, 1)
    for field, out in ((a, ga_out), (b, gb_out)):
        hi, lo = halves(flat(field))
        out[...] = dot(jnp.concatenate([hi, lo], 1), grad[...]) + dot(hi, grad_lo[...])
    hi, lo = halves(flat(ka))
    kg_out[...] = dot(jnp.concatenate([hi, lo], 1), pick[...])


def step_kernel(
    flip, odd, an, ap, bn, bp, ka, c, a0, b0, f1, ga, gb, kg0, far_in, near_in,
    first, first_lo, grad, second_a, ta_hi, ta_lo, tb_hi, tb_lo, t_both,
    k_out, al_out, bl_out, v2a, v1b, u1_out, kg,
    left, raw, u, ku, cu, qu, wa, wb, y1, v1a, k, sem,
):
    lane = lax.broadcasted_iota(jnp.int32, (YP, XL), 1)
    rows = slice(0, YP)
    sent = []

    def send(src, dst, dense):
        if dense:
            src, dst = src.at[:, rows, :], dst.at[:, :, 0, :]
        sent.append(pltpu.make_async_copy(src, dst, sem.at[len(sent)]))
        sent[-1].start()

    is_odd = odd[0] != 0
    raw[...] = jnp.where(is_odd, far_in[...], near_in[...])
    flip_rows(raw, left, flip[0])
    own_a = (lane & 63) < LANE_B
    for z in range(ZP):
        i, at = z % PLANES, GROUP * (z // PLANES)
        before = jnp.where(is_odd, near_in[i], far_in[i])
        if at:
            before = pltpu.roll(before, XL - at, 1)
        tile = jnp.where(lane < AFTER, before, pltpu.roll(left[i], (AFTER - at) % XL, 1))
        u[z, rows, :] = tile
        ku[z, rows, :] = jnp.where(
            own_a, pltpu.roll(tile, XL - LANE_K, 1), pltpu.roll(tile, XL - LANE_K + LANE_B, 1)
        )
        qu[z, rows, :] = pltpu.roll(tile, XL - LANE_PA, 1)
        cu[z, rows, :] = pltpu.roll(tile, XL - LANE_CA, 1)
    apply_y(((u, y1),), ku)

    def use(i, z, rows, value):
        qu[z, rows, :] = qu[z, rows, :] - cu[z, rows, :] * (y1[z, rows, :] + value)

    apply_z((u,), ku, use)

    lane2 = lax.broadcasted_iota(jnp.int32, (ROWS, XL), 1)
    tall = lambda value: value.reshape(ZP, YPAD, value.shape[-1])
    hi, lo = halves(flat(u))
    edge = dot(jnp.concatenate([hi, lo], 1), first[...]) + dot(hi, first_lo[...])
    kg[...] = jnp.concatenate([flat(ka), kg0[...] + edge[:, 4 * XL :]], 1)
    xa = dot3((ga[...] + edge[:, 0 : 2 * XL]) * kg[...], ta_hi[...], ta_lo[...])
    xb = dot3((gb[...] + edge[:, 2 * XL : 4 * XL]) * kg[...], tb_hi[...], tb_lo[...])
    u1 = flat(qu) - flat(cu) * (xa[:, XL:] + xb[:, XL:])
    hi = u1.astype(jnp.bfloat16).astype(jnp.float32)
    packed = jnp.where(
        (lane2 & 63) < 16,
        hi,
        jnp.where((lane2 & 63) < 32, pltpu.roll(u1 - hi, 16, 1), pltpu.roll(hi, 32, 1)),
    ).astype(jnp.bfloat16)
    u1_out[...] = packed
    wa[...] = tall(xa[:, 0:XL])
    wb[...] = tall(xb[:, 0:XL])
    for z in range(ZP):
        cz = c[z, rows, :]
        acc_a = a0[z, rows, :] - cz * wa[z, rows, :]
        acc_b = b0[z, rows, :] - cz * wb[z, rows, :]
        a, b = an[z, rows, :], bn[z, rows, :]
        v1a[z, rows, :] = 2.0 * a - ap[z, rows, :] + acc_a
        v1b[z, rows, :] = 2.0 * b - bp[z, rows, :] + acc_b
        ku[z, rows, :] = b * acc_a
    send(v1a, al_out, True)
    send(v1b, bl_out, True)
    apply_y(((v1a, y1),), ka)

    def add(i, z, rows, value):
        y1[z, rows, :] = y1[z, rows, :] + value

    apply_z((v1a,), ka, add)
    wa[...] = tall(second_x(v1a, packed, grad, second_a, kg, t_both))
    for i in (6, 7):
        k[72 * i + 64 : 72 * i + 72, :] = jnp.zeros((8, XL), jnp.float32)
    for z in (ZP - 1, *range(ZP - 1)):
        acc_a = f1[z, rows, :] - c[z, rows, :] * (wa[z, rows, :] + y1[z, rows, :])
        v2a[z, rows, :] = 2.0 * v1a[z, rows, :] - an[z, rows, :] + acc_a
        t = ku[z, rows, :] + v1b[z, rows, :] * acc_a
        if z < ZP - 1:
            at = 72 * (z // 2) + 32 * (z % 2)
            k[at : at + 8, :] = t[0:8]
            k[at + 8 : at + 16, :] = t[25:33]
            k[at + 16 : at + 24, :] = t[8:16]
            k[at + 24 : at + 32, :] = t[17:25]
        else:
            for i in range(4):
                at = 72 * i + 64
                k[at : at + 4, :] = t[4 * i : 4 * i + 4]
                k[at + 4 : at + 8, :] = t[29 - 4 * i : 33 - 4 * i]
        at = 72 * (4 + z // 8) + 64 + z % 8
        k[at : at + 1, :] = t[16:17]
        for j in {1: [0], 3: [1], 5: [2], 7: [3], 9: [4], 13: [6], 15: [5, 7]}.get(z, []):
            at = pl.ds(72 * j, 72)
            send(k.at[at], k_out.at[at], False)
    for copy in sent:
        copy.wait()


def second_x(v, packed, grad, second, kg, t_both):
    hi, lo = halves(flat(v))
    g = dot(jnp.concatenate([hi, lo], 1), grad[...])
    g = g + dot(jnp.concatenate([hi, packed], 1), second[...])
    hi, lo = halves(g * kg[...])
    both = dot(hi, t_both[...])
    return both[:, 0:XL] + both[:, XL:] + dot(lo, t_both[:, 0:XL])


def last_kernel(bn, ka, c, v1b, v2a, u1, kg, grad, second_b, t_both, af_out, bf_out, y1, wb, sem):
    rows = slice(0, YP)
    first = pltpu.make_async_copy(v2a.at[:, rows, :], af_out.at[:, :, 0, :], sem.at[1])
    first.start()
    apply_y(((v1b, y1),), ka)

    def add(i, z, rows, value):
        y1[z, rows, :] = y1[z, rows, :] + value

    apply_z((v1b,), ka, add)
    x = second_x(v1b, u1[...], grad, second_b, kg, t_both)
    wb[...] = x.reshape(ZP, YPAD, XL)
    for z in range(ZP):
        acc = c[z, rows, :] * (wb[z, rows, :] + y1[z, rows, :])
        wb[z, rows, :] = 2.0 * v1b[z, rows, :] - bn[z, rows, :] - acc
    copy = pltpu.make_async_copy(wb.at[:, rows, :], bf_out.at[:, :, 0, :], sem.at[0])
    copy.start()
    first.wait()
    copy.wait()


def turn(part, whole, flipped):
    for i in range(part // 72):
        for r in range(8):
            for j in range(9):
                at = 72 * i + 8 * (j ^ 1 if j < 8 else j) + 7 - r
                flipped[72 * i + 8 * j + r : 72 * i + 8 * j + r + 1, :] = whole[at : at + 1, :]


def turned_part(group, value, flipped):
    row = lax.broadcasted_iota(jnp.int32, value.shape, 0)
    stays = (row % 72 >= 64) & (row // 72 + group[0] * (value.shape[0] // 72) >= 4)
    return jnp.where(stays, value, flipped[...])


def sum_kernel(flip, group, odd, parts, far_out, near_out, own_out, flipped):
    total = parts[0]
    for i in range(1, parts.shape[0]):
        total = total + parts[i]
    own_out[...] = total
    turn(total.shape[0], own_out, flipped)
    other = turned_part(group, total, flipped)
    turned = flip[0] != 0
    far_out[...] = jnp.where(turned & (odd[0] != 0), other, total)
    near_out[...] = jnp.where(turned & (odd[0] == 0), other, total)


def smooth_kernel(flip, group, odd, far_in, own, near_in, gx_hi, gx_lo, out, done, flipped, sem):
    is_odd = odd[0] != 0
    before = jnp.where(is_odd, near_in[...], far_in[...])
    after = jnp.where(is_odd, far_in[...], near_in[...])
    done[...] = after
    turn(after.shape[0], done, flipped)
    after = jnp.where(flip[0] != 0, turned_part(group, after, flipped), after)
    total = None
    for i, part in enumerate((before, own[...], after)):
        at = slice(XL * i, XL * (i + 1))
        one = dot3(part, gx_hi[at, :], gx_lo[at, :])
        total = one if total is None else total + one
    done[...] = total
    copies = [pltpu.make_async_copy(done, out.at[i], sem.at[i]) for i in range(out.shape[0])]
    for copy in copies:
        copy.start()
    for copy in copies:
        copy.wait()


def finish_kernel(t, blocks_hi, blocks_lo, end_hi, end_lo, middle, out, rows, done_all, sem):
    def planes(first, n, m_hi, m_lo):
        if n > 1:
            for i in range(n):
                at = 72 * ((first + i) // 2) + 32 * (i % 2)
                rows[32 * i : 32 * i + 32, :] = t[at : at + 32, :]
        else:
            for i in range(4):
                rows[8 * i : 8 * i + 8, :] = t[72 * i + 64 : 72 * i + 72, :]
        hi, lo = halves(rows[0 : 32 * n, :])
        done = dot(m_hi[...], hi) + dot(m_hi[...], lo) + dot(m_lo[...], hi)
        for i in range(n):
            z = first + i
            at = 72 * (4 + z // 8) + 64 + z % 8
            done_all[z] = done[i * YPAD : (i + 1) * YPAD] + middle[...] * t[at : at + 1, :]
        at = pl.ds(first, n)
        copy = pltpu.make_async_copy(done_all.at[at, 0:YP, :], out.at[at], sem.at[first // 8])
        copy.start()
        return copy

    copies = [planes(0, 8, blocks_hi, blocks_lo), planes(8, 8, blocks_hi, blocks_lo), planes(16, 1, end_hi, end_lo)]
    for copy in copies:
        copy.wait()


SMEM_SPEC = pl.BlockSpec(memory_space=pltpu.SMEM)
VMEM_SPEC = pl.BlockSpec(memory_space=pltpu.VMEM)
ANY_SPEC = pl.BlockSpec(memory_space=pl.ANY)


def near(*shape, dtype=jnp.float32):
    return pltpu.VMEM(shape, dtype)


def distant(*shape, dtype=jnp.float32):
    return pltpu.HBM(shape, dtype)


def call(kernel, outs, scalars, arrays, scratch=(), far=(), flops=0, moved=0, limit=24):
    far = [pltpu.with_memory_space_constraint(v, pltpu.HBM) for v in far]
    out_specs = [ANY_SPEC if o.memory_space == pltpu.HBM else VMEM_SPEC for o in outs]
    return pl.pallas_call(
        kernel,
        out_shape=outs,
        in_specs=[SMEM_SPEC] * len(scalars) + [VMEM_SPEC] * len(arrays) + [ANY_SPEC] * len(far),
        out_specs=out_specs,
        scratch_shapes=list(scratch),
        compiler_params=pltpu.CompilerParams(vmem_limit_bytes=limit * 1024 * 1024),
        cost_estimate=pl.CostEstimate(flops=flops, bytes_accessed=moved, transcendentals=0),
    )(*scalars, *arrays, *far)


def swap(value, odd):
    n = lax.axis_size("cuts")
    return lax.ppermute(value, "cuts", [(i, (i + 1 if i % 2 == odd else i - 1) % n) for i in range(n)])


def local(an, ap, bn, bp, kappa, density, flip, index, source):
    dense, padded, edge = distant(ZP, YP, 1, XL), near(ZP, YPAD, XL), near(PLANES, YP, XL)
    odd = (lax.axis_index("cuts").astype(jnp.int32) % 2).reshape(1)
    src = source[0]
    tab = {name: jnp.asarray(value) for name, value in tables().items()}
    fields = [v.reshape(ZP, YP, 1, XL) for v in (an, bn, ap, bp)]
    dma = pltpu.SemaphoreType.DMA
    receivers = [pltpu.SMEM(v.shape, v.dtype) for v in (index, src)]
    to_far, to_near, an, bn, ap, bp, ka, c, f0 = call(
        pack_kernel,
        [edge, edge] + [padded] * 7,
        [flip, odd],
        [],
        [padded, edge, edge, *receivers, dma((8,))],
        far=[*fields, kappa, density, index, src],
        moved=4_000_000,
    )
    from_far = swap(to_far, 1)
    wide, narrow = near(ROWS, 2 * XL), near(ROWS, XL)
    from_near = swap(to_near, 0)
    a0, b0, f1, ga, gb, kg0 = call(
        local_kernel,
        [padded, padded, padded, wide, wide, narrow],
        [],
        [an, bn, ka, c, f0, tab["grad"], tab["grad_lo"], tab["pick"]],
        [*receivers, dma((2,))],
        far=[index, src],
        flops=300_000_000,
        moved=5_000_000,
    )
    packed = near(ROWS, XL, dtype=jnp.bfloat16)
    k, al, bl, v2a, v1b, u1, kg = call(
        step_kernel,
        [distant(KROWS, XL), dense, dense, padded, padded, packed, wide],
        [flip, odd],
        [an, ap, bn, bp, ka, c, a0, b0, f1, ga, gb, kg0, from_far, from_near]
        + [tab[n] for n in ("first", "first_lo", "grad", "second_a", "ta_hi", "ta_lo", "tb_hi", "tb_lo", "t_both")],
        [edge, edge] + [padded] * 8 + [near(KROWS, XL), dma((10,))],
        flops=600_000_000,
        moved=6_000_000,
    )
    groups = lax.axis_size("event")
    part = KROWS // groups
    parts = lax.all_to_all(k.reshape(groups, part, XL), "event", 0, 0)
    af, bf = call(
        last_kernel,
        [dense, dense],
        [],
        [bn, ka, c, v1b, v2a, u1, kg, tab["grad"], tab["second_b"], tab["t_both"]],
        [padded, padded, dma((2,))],
        flops=300_000_000,
        moved=5_000_000,
    )
    outs = (af, al, bf, bl)
    group = lax.axis_index("event").astype(jnp.int32).reshape(1)
    place = [flip, group, odd]
    to_far, to_near, total = call(sum_kernel, [near(part, XL)] * 3, place, [parts], [near(part, XL)])
    from_near = swap(to_near, 0)
    from_far = swap(to_far, 1)
    gauss_x, gauss_y = smoothing_tables()
    gauss = [jnp.asarray(v) for v in split(gauss_x)]
    spread = call(
        smooth_kernel,
        [distant(groups, part, XL)],
        place,
        [from_far, total, from_near, *gauss],
        [near(part, XL), near(part, XL), dma((8,))],
    )[0]
    whole = lax.all_to_all(spread, "event", 0, 0).reshape(KROWS, XL)
    order = [*range(0, 8), *range(25, 33), *range(8, 16), *range(17, 25)]
    blocks, end, middle = np.zeros((8 * YPAD, 256)), np.zeros((YPAD, 32)), np.zeros((YPAD, XL))
    for i in range(8):
        blocks[i * YPAD : i * YPAD + YP, i * 32 : i * 32 + 32] = gauss_y[:, order]
    end[0:YP] = gauss_y[:, [y for i in range(0, 16, 4) for y in (*range(i, i + 4), *range(29 - i, 33 - i))]]
    middle[0:YP] = gauss_y[:, 16:17]
    smoothed = call(
        finish_kernel,
        [distant(ZP, YP, XL)],
        [],
        [whole, *(jnp.asarray(v) for v in (*split(blocks), *split(end))), jnp.asarray(middle, jnp.float32)],
        [near(256, XL), near(ZP, YPAD, XL), dma((3,))],
    )[0]
    return *(v.reshape(1, ZP, YP, XL) for v in outs), smoothed


def solution(mesh):
    field = P("event", None, None, "cuts")
    grid = P(None, None, "cuts")
    return jax.shard_map(
        local,
        mesh=mesh,
        in_specs=(field,) * 4 + (grid, grid, P("cuts"), P("cuts"), P("event", None, "cuts")),
        out_specs=(field,) * 4 + (grid,),
        check_vma=False,
    )
```
